32 devices in a mesh: graph: 2 (over x), feat: 16 (over z, y, core).
Axes of the slice: x: 2, y: 2, z: 4, core: 2. Of those that a mesh axis runs over, the one named last changes fastest.
Arguments:
- features: bfloat16 [2048, 512], P('graph', 'feat'), may hold values from -6 to 6
- w_first: bfloat16 [2, 512, 256], P(None, 'feat'), may hold values from -0.25 to 0.25
- w_second: bfloat16 [2, 256, 256], replicated, may hold values from -0.375 to 0.375
- cotangent: bfloat16 [1024, 256], P(('graph', 'feat')), may hold values from -6 to 6
- nbr_first: int32 [1024, 15], P('graph'), may hold values from 0 to 1023
- send_rows: int32 [32, 2, 8], P(('graph', 'feat')), may hold values from -1 to 31, as said below
- nbr_second: int32 [1024, 10], P(('graph', 'feat')), may hold values from 0 to 47, as said below
Outputs:
- layer_out: bfloat16 [1024, 256], P(('graph', 'feat'))
- grad_second: float32 [2, 256, 256], replicated
- grad_first: float32 [2, 512, 256], P(None, 'feat')
The draws below stay inside these ranges and needn't reach their ends.
Inputs may be any that keep to these rules, and one draw needn't show every extreme that they name: `send_rows`: for each device and partition the used slots come first; a device's own partition gets only -1; every used slot of a device to one partition names a different row; for each feat index some partition other than the last receives all 8 slots used from every other partition. `nbr_second`: each entry below 32 names an owned row; every other entry names a used slot received from another partition.
All inputs are finite; a program needn't handle non-finite values.
Results may differ from the reference program's by a relative error of at most 0.0051.
Values may be sent and summed in bfloat16 or wider, within the bound.
No kernel may reach another device: no remote copies, remote signals or barrier semaphores. Data moves between devices by JAX's collectives and lax.ppermute only.
A program may use at most 64 MiB of HBM per device.

```python
import jax
import jax.numpy as jnp
from jax import lax

F = 512
HID = 256
FAN1 = 15
FAN2 = 10
OWN = 32
HALO = 8
ROWS_G = 512
SRC_G = 1024
N_GRAPH = 2
N_FEAT = 16


def halo_counts(key):
    key = jax.random.fold_in(key, 101)
    key_one, key_two, key_hot = jax.random.split(key, 3)
    shape = (N_FEAT, N_GRAPH, N_GRAPH)
    first = jax.random.randint(key_one, shape, 1, HALO + 1)
    second = jax.random.randint(key_two, shape, 1, HALO + 1)
    base = jnp.minimum(first, second)
    hot = jax.random.randint(key_hot, (N_FEAT,), 0, N_GRAPH - 1)
    receiver = jnp.arange(N_GRAPH)
    full = receiver[None, None, :] == hot[:, None, None]
    counts = jnp.where(full, HALO, base)
    sender = jnp.arange(N_GRAPH)[None, :, None]
    return (jnp.where(sender == receiver[None, None, :], 0, counts), hot)


def draw_send_rows(key, part):
    counts, hot = halo_counts(key)
    key = jax.random.fold_in(key, 1)
    key_start, key_stride = jax.random.split(key)
    shape = (N_GRAPH, N_FEAT, N_GRAPH, 1)
    start = jax.random.randint(key_start, shape, 0, OWN)
    graph_ix = jnp.arange(N_GRAPH)[:, None, None, None]
    peer_ix = jnp.arange(N_GRAPH)[None, None, :, None]
    start = jnp.where(peer_ix == (graph_ix + 1) % N_GRAPH, OWN - 1, start)
    stride = 2 * jax.random.randint(key_stride, shape, 0, max(OWN // 2, 1)) + 1
    slots = jnp.arange(HALO)[None, None, None, :]
    rows = (start + slots * stride) % OWN
    used = jnp.transpose(counts, (1, 0, 2))[..., None] > slots
    return jnp.where(used, rows, -1).reshape(N_GRAPH * N_FEAT, N_GRAPH, HALO).astype(jnp.int32)


def draw_nbr_second(key, part):
    counts, hot = halo_counts(key)
    key = jax.random.fold_in(key, 2)
    key_local, key_coin, key_peer, key_slot = jax.random.split(key, 4)
    shape = (N_GRAPH, N_FEAT, OWN, FAN2)
    local = jax.random.randint(key_local, shape, 0, OWN)
    coin = jax.random.randint(key_coin, shape, 0, 2)
    graph_ix = jnp.arange(N_GRAPH)[:, None, None, None]
    feat_ix = jnp.arange(N_FEAT)[None, :, None, None]
    peer = (graph_ix + 1 + jax.random.randint(key_peer, shape, 0, N_GRAPH - 1)) % N_GRAPH
    have = counts[feat_ix, peer, graph_ix]
    slot = jax.random.randint(key_slot, shape, 0, 1 << 20) % have
    far = OWN + peer * HALO + slot
    result = jnp.where(coin == 0, local, far)
    row_ix = jnp.arange(OWN)[None, None, :, None]
    k_ix = jnp.arange(FAN2)[None, None, None, :]
    is_hot = graph_ix == hot[None, :, None, None]
    result = jnp.where(is_hot & (row_ix == 0) & (k_ix == 0), OWN + N_GRAPH * HALO - 1, result)
    result = jnp.where(is_hot & (row_ix == 0) & (k_ix == 1), 0, result)
    return result.reshape(N_GRAPH * N_FEAT * OWN, FAN2).astype(jnp.int32)


def place_ends(values, rng, least, top_value):
    longest = values.shape.index(max(values.shape))
    spots = []
    for shift in (0, 1):
        where = [jax.random.randint(jax.random.fold_in(rng, axis), (), 0, length) for axis, length in enumerate(values.shape)]
        where[longest] = (where[longest] + shift) % values.shape[longest]
        spots.append(tuple(where))
    return values.at[spots[0]].set(least).at[spots[1]].set(top_value)


def levels(rng, dims, shards, low, top_value):
    def one(position, shards_of):
        draws = jax.random.uniform(jax.random.fold_in(jax.random.fold_in(rng, 6), position), (shards_of,), jnp.float32, low / len(shards), top_value / len(shards))
        return jnp.repeat(jnp.exp(draws), dims[position] // shards_of).reshape((-1,) + (1,) * (len(dims) - position - 1))

    gain = one(*shards[0])
    for cut in shards[1:]:
        gain = gain * one(*cut)
    return gain


def bell_draw(key, extent, spread, most, cuts=(), dtype=jnp.bfloat16):
    array = jax.random.normal(key, extent, jnp.float32) * spread
    if len(cuts) > 0:
        array = levels(key, extent, cuts, -0.22, 0.18) * array
    return jnp.clip(array, min=-most, max=most).astype(dtype)


def setup_inputs(seed: int = 0) -> dict:
    key_list = jax.random.split(jax.random.key(seed), 8)
    return {
        "features": bell_draw(key_list[0], (N_GRAPH * SRC_G, F), 1.0, 6.0, ((0, 2), (1, 16))),
        "w_first": bell_draw(key_list[1], (2, F, HID), F ** -0.5, 0.25, ((1, 16),)),
        "w_second": bell_draw(key_list[2], (2, HID, HID), HID ** -0.5, 0.375),
        "cotangent": bell_draw(key_list[3], (N_GRAPH * ROWS_G, HID), 1.0, 6.0, ((0, 32),)),
        "nbr_first": place_ends(jax.random.randint(key_list[4], (N_GRAPH * ROWS_G, FAN1), 0, SRC_G), jax.random.fold_in(key_list[4], 1), 0, SRC_G - 1).astype(jnp.int32),
        "send_rows": draw_send_rows(jax.random.fold_in(key_list[7], 71), 0),
        "nbr_second": draw_nbr_second(jax.random.fold_in(key_list[7], 71), 0),
    }


def silu_grad(value):
    sig = jax.nn.sigmoid(value)
    return sig * (1.0 + value * (1.0 - sig))

def reference(features, w_first, w_second, cotangent, nbr_first, send_rows, nbr_second):
    high = lax.Precision.HIGHEST
    feats = features.reshape(N_GRAPH, SRC_G, F)
    nbrs = nbr_first.reshape(N_GRAPH, ROWS_G, FAN1)

    def first(args):
        source, near = args
        gathered = source[near].astype(jnp.float32)
        mean_one = (lax.optimization_barrier(jnp.sum(gathered, axis=1)) / FAN1).astype(jnp.bfloat16)
        pre = jnp.dot(source[:ROWS_G], w_first[0], preferred_element_type=jnp.float32)
        pre = pre + jnp.dot(mean_one, w_first[1], preferred_element_type=jnp.float32)
        return (pre, mean_one)
    pre_one, mean_one = lax.map(first, (feats, nbrs))
    hidden = jax.nn.silu(pre_one).astype(jnp.bfloat16)
    h_dev = hidden.reshape(N_GRAPH, N_FEAT, OWN, HID)
    sends = send_rows.reshape(N_GRAPH, N_FEAT, N_GRAPH, HALO)
    recv_idx = jnp.transpose(sends, (2, 1, 0, 3))
    peer_ix = jnp.arange(N_GRAPH)[None, None, :, None]
    feat_ix = jnp.arange(N_FEAT)[None, :, None, None]
    halo = h_dev[peer_ix, feat_ix, jnp.maximum(recv_idx, 0)]
    halo = jnp.where((recv_idx >= 0)[..., None], halo, jnp.zeros_like(halo))
    ext = jnp.concatenate([h_dev, halo.reshape(N_GRAPH, N_FEAT, N_GRAPH * HALO, HID)], axis=2)
    width = OWN + N_GRAPH * HALO
    near_two = nbr_second.reshape(N_GRAPH, N_FEAT, OWN, FAN2)
    counts = jnp.zeros((N_GRAPH, N_FEAT, OWN, width), jnp.float32)
    for k in range(FAN2):
        counts = counts + (near_two[..., k, None] == jnp.arange(width)[None, None, None, :]).astype(jnp.float32)
    mean_two = (jnp.einsum('gfij,gfjh->gfih', counts, ext.astype(jnp.float32), precision=high) / FAN2).astype(jnp.bfloat16)
    w_two = w_second.astype(jnp.float32)
    out = jnp.einsum('gfih,ho->gfio', h_dev.astype(jnp.float32), w_two[0], precision=high)
    out = out + jnp.einsum('gfih,ho->gfio', mean_two.astype(jnp.float32), w_two[1], precision=high)
    layer_out = out.astype(jnp.bfloat16).reshape(N_GRAPH * ROWS_G, HID)
    cot = cotangent.reshape(N_GRAPH, N_FEAT, OWN, HID).astype(jnp.float32)
    grad_self = jnp.einsum('gfih,gfio->ho', h_dev.astype(jnp.float32), cot, precision=high)
    grad_near = jnp.einsum('gfih,gfio->ho', mean_two.astype(jnp.float32), cot, precision=high)
    grad_second = jnp.stack([grad_self, grad_near])
    d_self = jnp.einsum('gfio,ho->gfih', cot, w_two[0], precision=high)
    d_mean = jnp.einsum('gfio,ho->gfih', cot, w_two[1], precision=high) / FAN2
    d_ext = jnp.einsum('gfij,gfih->gfjh', counts, d_mean, precision=high)
    halo_grad = d_ext[:, :, OWN:].reshape(N_GRAPH, N_FEAT, N_GRAPH, HALO, HID).astype(jnp.bfloat16)
    back = jnp.transpose(halo_grad, (2, 1, 0, 3, 4)).astype(jnp.float32)
    onehot = (sends[..., None] == jnp.arange(OWN)[None, None, None, None, :]).astype(jnp.float32)
    d_back = jnp.einsum('pfqsr,pfqsh->pfrh', onehot, back, precision=high)
    d_hidden = d_self + d_ext[:, :, :OWN] + d_back
    pre_dev = pre_one.reshape(N_GRAPH, N_FEAT, OWN, HID)
    d_pre = (d_hidden * silu_grad(pre_dev)).astype(jnp.bfloat16).reshape(N_GRAPH, ROWS_G, HID)
    d_pre32 = d_pre.astype(jnp.float32)
    grad_one = jnp.einsum('grf,grh->fh', feats[:, :ROWS_G].astype(jnp.float32), d_pre32, precision=high)
    grad_two = jnp.einsum('grf,grh->fh', mean_one.astype(jnp.float32), d_pre32, precision=high)
    grad_first = jnp.stack([grad_one, grad_two])
    return (layer_out, grad_second, grad_first)
```

```python
import functools

import jax
import jax.numpy as jnp
from jax import lax
from jax.experimental import pallas as pl
from jax.experimental.pallas import tpu as pltpu
from jax.sharding import PartitionSpec as P

HID = 256
FAN1 = 15
FAN2 = 10
OWN = 32
HALO = 8
LANES = 128
INTS = 16
F32 = jnp.float32
BF16 = jnp.bfloat16
AXES = ("graph", "feat")
PLANE = ((0, 0), (1, 0), (0, 1), (1, 1))


def silu_grad(value):
    sig = jax.nn.sigmoid(value)
    return sig * (1.0 + value * (1.0 - sig))


def dot(a, b, contract):
    return lax.dot_general(a, b, (contract, ((), ())), preferred_element_type=F32)


def write_pack(sends, cot, near, pack):
    my_z = lax.axis_index("feat") // 4
    for side in range(2):
        pack[side * OWN : (side + 1) * OWN, :] = cot[:, side * LANES : (side + 1) * LANES]
    lane = lax.broadcasted_iota(jnp.int32, (INTS, LANES), 1)
    row = lax.broadcasted_iota(jnp.int32, (INTS, LANES), 0)
    lists = jnp.concatenate([near[...], jnp.zeros((INTS - FAN2, OWN), jnp.int32)], axis=0)
    ints = jnp.where(lane // OWN == my_z, jnp.concatenate([lists] * (LANES // OWN), axis=1), 0)
    for g in range(2):
        for s in range(HALO):
            here = (row == FAN2) & (lane == my_z * OWN + g * HALO + s)
            ints = jnp.where(here, sends[0, g, s], ints)
    pack[2 * OWN : 2 * OWN + INTS, :] = ints.astype(F32).astype(BF16)


def first_kernel(
    feat_hbm, nbr_hbm, w_hbm, cot_hbm, near_hbm, sends_hbm, pack, x_t, kept, sent,
    feat_t, nbr_t, w_first, cot, near, sends, share, sems,
):
    pairs = ((nbr_hbm, nbr_t), (feat_hbm, feat_t), (w_hbm, w_first), (cot_hbm, cot), (near_hbm, near), (sends_hbm, sends))
    copies = [pltpu.make_async_copy(src, dst, sems.at[i]) for i, (src, dst) in enumerate(pairs)]
    for copy in copies:
        copy.start()
    copies[0].wait()
    copies[1].wait()
    sources = feat_t.shape[1]
    row = lax.broadcasted_iota(jnp.int32, (LANES, LANES), 0)
    for t in range(x_t.shape[0]):
        cols = slice(t * LANES, (t + 1) * LANES)
        low = nbr_t[:, cols] & (LANES - 1)
        unit = jnp.left_shift(1, 4 * jnp.right_shift(nbr_t[:, cols], 7))
        packed = jnp.zeros((LANES, LANES), jnp.int32)
        for k in range(FAN1):
            packed = packed + jnp.where(row == low[k : k + 1, :], unit[k : k + 1, :], 0)
        parts = [jnp.right_shift(packed, 4 * b) & 15 for b in range(sources // LANES)]
        counts = jnp.concatenate([part.astype(F32).astype(BF16) for part in parts], axis=0)
        mean = (dot(feat_t[...], counts, ((1,), (0,))) / FAN1).astype(BF16)
        chunk = jnp.concatenate([feat_t[:, cols], mean], axis=0)
        x_t[t] = chunk
        sent[2 * x_t.shape[0] + t] = chunk
        if t == 0:
            copies[2].wait()
        share[cols, :] = dot(chunk, w_first[...], ((0,), (0,)))
    line = x_t.shape[0]
    my_feat = lax.axis_index("feat")
    for c, out in enumerate((kept, sent)):
        for y in range(2):
            for z in range(line):
                owner = z * 4 + ((my_feat % 4) ^ (2 * y + c))
                block = share[pl.ds(pl.multiple_of(owner * OWN, OWN), OWN), :].astype(out.dtype)
                for side in range(2):
                    out[y * line + z, side * OWN : (side + 1) * OWN, :] = block[:, side * LANES : (side + 1) * LANES]
    for copy in copies[3:]:
        copy.wait()
    write_pack(sends, cot, near, pack)


def sum_core_kernel(mine, received, kept, sent):
    line = kept.shape[0]
    kept[...] = mine[0:line] + received[0:line].astype(F32)
    sent[...] = (mine[line : 2 * line] + received[line : 2 * line].astype(F32)).astype(BF16)


def sum_plane_kernel(pack, mine, received, message):
    total = (mine[...] + received[...].astype(F32)).astype(BF16)
    rows = total.shape[0] * total.shape[1]
    message[0:rows, :] = total.reshape(rows, LANES)
    message[rows:, :] = pack[...]


def sum_line_kernel(after, *refs):
    parts, (exact, message) = refs[:-2], refs[-2:]
    my_z = lax.axis_index("feat") // 4
    line, width = exact.shape[0], exact.shape[1]
    rows = line * width
    sums = [part[0:rows, :].astype(F32) for part in parts]
    while len(sums) > 1:
        sums = [a + b for a, b in zip(sums[::2], sums[1::2])]
    total = sums[0].reshape(exact.shape)
    exact[...] = total
    total = total.astype(BF16)
    for z, part in enumerate(parts):
        message[2 * z * width : (2 * z + 1) * width, :] = total[z]
        at = pl.multiple_of((2 * (my_z ^ z) + 1) * width, width)
        message[pl.ds(at, width), :] = part[rows : rows + width, :]
    lists = [part[rows + width :, :].astype(F32) for part in parts]
    message[2 * rows :, :] = functools.reduce(lambda a, b: a + b, lists).astype(BF16)


def back_kernel(n_feat, plane_0, plane_1, plane_2, plane_3, w_second, cot_all, near_cot, d_hidden, own_counts, lists, spread, turn):
    line = n_feat // 4
    width = 2 * OWN
    my_graph = lax.axis_index("graph")
    my_z = lax.axis_index("feat") // 4
    my_y = lax.axis_index("feat") // 2 % 2
    for (x, y), message in zip(PLANE, (plane_0, plane_1, plane_2, plane_3)):
        at = (my_graph ^ x) * 2 + (my_y ^ y)
        lists[at] = message[2 * line * width :, :]
        for z in range(line):
            span = pl.ds(pl.multiple_of(at * LANES + z * OWN, OWN), OWN)
            for side in range(2):
                top = (2 * z + 1) * width + side * OWN
                cot_all[span, side * LANES : (side + 1) * LANES] = message[top : top + OWN, :]

    ints = lists[...].reshape(4 * INTS, LANES)
    source = lax.broadcasted_iota(jnp.int32, (LANES, LANES), 0)
    start = lax.broadcasted_iota(jnp.int32, (LANES, LANES), 1) // OWN * OWN
    pick = jnp.concatenate([jnp.where(source == start + s, 1.0, 0.0).astype(BF16) for s in range(2 * HALO)], axis=1)
    sent = dot(ints, pick, ((1,), (0,)))

    z_of = lax.broadcasted_iota(jnp.int32, (width, LANES), 1) // OWN
    slot_ix = lax.broadcasted_iota(jnp.int32, (width, LANES), 0).astype(F32)
    for y in range(2):
        total = jnp.zeros((line * width, HID), F32)
        for g in range(2):
            at = g * 2 + y
            entries = ints[at * INTS : (at + 1) * INTS, :].astype(F32)
            place_of = entries + float(g * OWN)
            for p in range(2):
                for s in range(HALO):
                    row = (p * 2 + y) * INTS + FAN2
                    there = sent[row : row + 1, (g * HALO + s) * LANES : (g * HALO + s + 1) * LANES] + p * OWN
                    place_of = jnp.where(entries == float(OWN + p * HALO + s), there, place_of)
            counts = jnp.zeros((width, LANES), F32)
            for k in range(FAN2):
                counts = counts + jnp.where(slot_ix == place_of[k : k + 1, :], 1.0, 0.0)
            spread[at] = counts
            block = jnp.concatenate([jnp.where(z_of == z, counts, 0.0) for z in range(line)], axis=0).astype(BF16)
            total = total + dot(block, cot_all[at * LANES : (at + 1) * LANES, :], ((1,), (0,)))
        total = (total / FAN2).astype(BF16)
        for z in range(line):
            for p in range(2):
                at = (p * 2 + y) * LANES + z * OWN
                near_cot[at : at + OWN, :] = total[z * width + p * OWN : z * width + (p + 1) * OWN, :]

    turn[...] = spread[pl.ds(my_graph * 2 + my_y, 1)][0].T
    own_counts[...] = turn[pl.ds(pl.multiple_of(my_z * OWN, OWN), OWN), :]

    part = dot(cot_all[...], w_second[0], ((1,), (1,)))
    d_hidden[...] = part + dot(near_cot[...], w_second[1], ((1,), (1,)))


def last_kernel(
    n_feat, plane_0, plane_1, plane_2, plane_3, exact, cot, near_cot, d_hidden, own_counts, x_mine, x_core, x_peer, x_last, w_second,
    layer_out, swapped, kept, hidden, d_pre, slices, ext,
):
    my_graph = lax.axis_index("graph")
    my_feat = lax.axis_index("feat")
    rows = n_feat * OWN
    half = rows // 2
    line = n_feat // 4
    d_pre[...] = jnp.zeros_like(d_pre)
    my_y = my_feat // 2 % 2
    for (x, y), message in zip(PLANE, (plane_0, plane_1, plane_2, plane_3)):
        graph = my_graph ^ x
        for z in range(line):
            span = pl.ds(pl.multiple_of((graph * 2 + (my_y ^ y)) * LANES + z * OWN, OWN), OWN)
            top = 4 * z * OWN
            value = jnp.concatenate([message[top : top + OWN, :], message[top + OWN : top + 2 * OWN, :]], axis=1).astype(F32)
            sig = 0.5 + 0.5 * jnp.tanh(0.5 * value)
            hidden[span, :] = (value * sig).astype(BF16)
            slope = sig * (1.0 + value * (1.0 - sig))
            target = pl.ds(pl.multiple_of(graph * rows + (z * 4 + (my_feat % 4 ^ 2 * y)) * OWN, OWN), OWN)
            d_pre[target, :] = (d_hidden[span, :] * slope).astype(BF16)

    swapped[0:HID, :] = dot(hidden[...], cot[...], ((0,), (0,))).astype(BF16)
    swapped[HID : 2 * HID, :] = dot(hidden[...], near_cot[...], ((0,), (0,))).astype(BF16)

    for z in range(line):
        cols = slice(z * LANES, (z + 1) * LANES)
        slices[0, 0 : 2 * OWN, cols] = x_mine[z]
        slices[0, 2 * OWN : 4 * OWN, cols] = x_core[2 * line + z]
        slices[1, 0 : 2 * OWN, cols] = x_peer[z]
        slices[1, 2 * OWN : 4 * OWN, cols] = x_last[z]
    mine = d_pre[pl.ds(pl.multiple_of(my_graph * rows, rows), rows), :]
    peer = d_pre[pl.ds(pl.multiple_of((1 - my_graph) * rows, rows), rows), :]
    first = dot(slices[0], mine, ((1,), (0,))) + dot(slices[1], peer, ((1,), (0,)))
    kept[...] = first[0 : 2 * OWN, :]
    swapped[2 * HID : 2 * HID + 2 * OWN, :] = first[2 * OWN : 4 * OWN, :].astype(BF16)

    value = exact[pl.ds(my_feat // 4, 1)][0]
    value = jnp.concatenate([value[0:OWN, :], value[OWN : 2 * OWN, :]], axis=1)
    hidden_own = (value * (0.5 + 0.5 * jnp.tanh(0.5 * value))).astype(BF16)
    for p in range(2):
        at = (p * 2 + my_y) * LANES + (my_feat // 4) * OWN
        ext[p * OWN : (p + 1) * OWN, :] = hidden[pl.ds(pl.multiple_of(at, OWN), OWN), :]
    ext[pl.ds(pl.multiple_of(my_graph * OWN, OWN), OWN), :] = hidden_own
    mean = (dot(own_counts[...].astype(BF16), ext[...], ((1,), (0,))) / FAN2).astype(BF16)
    out = dot(hidden_own, w_second[0], ((1,), (0,))) + dot(mean, w_second[1], ((1,), (0,)))
    layer_out[...] = out.astype(BF16)


def add_kernel(mine, theirs, kept, grad_second, grad_first):
    for w in range(2):
        span = slice(w * HID, (w + 1) * HID)
        grad_second[w] = mine[span, :].astype(F32) + theirs[span, :].astype(F32)
    grad_first[...] = kept[...] + theirs[2 * HID : 2 * HID + 2 * OWN, :].astype(F32)


VMEM = pl.BlockSpec(memory_space=pltpu.VMEM)
ANY = pl.BlockSpec(memory_space=pl.ANY)
SMEM = pl.BlockSpec(memory_space=pltpu.SMEM)
LIMIT = 40 * 1024 * 1024


def call(kernel, outs, ins, scratch=(), name=None, aliases=None):
    return pl.pallas_call(
        kernel,
        out_shape=[jax.ShapeDtypeStruct(shape, dtype) for shape, dtype in outs],
        in_specs=ins,
        out_specs=[VMEM] * len(outs),
        scratch_shapes=list(scratch),
        input_output_aliases=aliases or {},
        compiler_params=pltpu.CompilerParams(vmem_limit_bytes=LIMIT),
        name=name,
    )


def swap(n_feat, value, relative):
    return lax.ppermute(value, AXES, [(d, d ^ relative) for d in range(2 * n_feat)])


def pair_body(n_feat, features, w_first, w_second, cotangent, nbr_first, send_rows, nbr_second):
    devices = 2 * n_feat
    rows = n_feat * OWN
    width = 2 * OWN
    line = n_feat // 4
    from_hbm = [features.T, nbr_first.T, w_first.reshape(width, HID), cotangent, nbr_second.T, send_rows]
    block = (line, width, LANES)
    pack, x_mine, kept, sent = call(
        first_kernel,
        [((width + INTS, LANES), BF16), (block, BF16), ((2 * line, width, LANES), F32), ((3 * line, width, LANES), BF16)],
        [ANY] * 6,
        [pltpu.VMEM(x.shape, x.dtype) for x in from_hbm[:-1]]
        + [pltpu.SMEM(send_rows.shape, jnp.int32), pltpu.VMEM((rows, HID), F32), pltpu.SemaphoreType.DMA((6,))],
        name="first",
    )(*[pltpu.with_memory_space_constraint(x, pltpu.HBM) for x in from_hbm])
    x_core = swap(n_feat, sent, 1)
    kept, sent = call(sum_core_kernel, [(block, F32), (block, BF16)], [VMEM] * 2, name="sum_core")(kept, x_core)
    x_peer = swap(n_feat, x_mine, n_feat)
    (message,) = call(
        sum_plane_kernel,
        [((line * width + width + INTS, LANES), BF16)],
        [VMEM] * 3,
        name="sum_plane",
    )(pack, kept, swap(n_feat, sent, 2))
    x_last = swap(n_feat, x_peer, 1)
    exact, message = call(
        sum_line_kernel,
        [(block, F32), ((2 * line * width + INTS, LANES), BF16)],
        [ANY] + [VMEM] * line,
        name="sum_line",
    )(x_peer, message, *[swap(n_feat, message, 4 * z) for z in range(1, line)])
    plane = [swap(n_feat, message, r) for r in (n_feat + 2, 2, n_feat)]
    plane = [message, *plane[::-1]]

    half = (devices // 2) * OWN
    cot, near_cot, d_hidden, own_counts = call(
        functools.partial(back_kernel, n_feat),
        [((half, HID), BF16), ((half, HID), BF16), ((half, HID), F32), ((OWN, width), F32)],
        [VMEM] * 5,
        [
            pltpu.VMEM((4, INTS, LANES), BF16),
            pltpu.VMEM((4, width, LANES), F32),
            pltpu.VMEM((LANES, width), F32),
        ],
        name="back",
    )(*plane, w_second)

    layer_out, swapped, kept = call(
        functools.partial(last_kernel, n_feat),
        [((OWN, HID), BF16), ((2 * HID + width, HID), BF16), ((width, HID), F32)],
        [VMEM] * 14,
        [
            pltpu.VMEM((half, HID), BF16),
            pltpu.VMEM((2 * half, HID), BF16),
            pltpu.VMEM((2, 2 * width, rows), BF16),
            pltpu.VMEM((width, HID), BF16),
        ],
        name="last",
    )(*plane, exact, cot, near_cot, d_hidden, own_counts, x_mine, x_core, x_peer, x_last, w_second)
    grad_second, grad_first = call(
        add_kernel,
        [((2, HID, HID), F32), ((width, HID), F32)],
        [VMEM] * 3,
        name="add",
    )(swapped, swap(n_feat, swapped, 1), kept)
    return (layer_out, grad_second, grad_first.reshape(2, OWN, HID))


def body(features, w_first, w_second, cotangent, nbr_first, send_rows, nbr_second):
    high = lax.Precision.HIGHEST
    targets = nbr_first.shape[0]
    gathered = features[nbr_first].astype(F32)
    mean_all = (jnp.sum(gathered, axis=1) / FAN1).astype(BF16)
    self_all = features[:targets]
    term = jnp.dot(self_all, w_first[0], preferred_element_type=F32)
    pre_one = lax.psum_scatter(
        term + jnp.dot(mean_all, w_first[1], preferred_element_type=F32),
        "feat",
        scatter_dimension=0,
        tiled=True,
    )
    hidden = jax.nn.silu(pre_one).astype(BF16)
    slot_rows = send_rows[0]
    valid = (slot_rows >= 0)[..., None]
    picked = hidden[jnp.maximum(slot_rows, 0)]
    outgoing_rows = jnp.where(valid, picked, jnp.zeros_like(picked))
    received = lax.all_to_all(outgoing_rows, "graph", split_axis=0, concat_axis=0, tiled=True)
    ext = jnp.concatenate([hidden, received.reshape(-1, HID)], axis=0)
    width = ext.shape[0]
    counts = jnp.zeros((OWN, width), F32)
    for k in range(FAN2):
        counts = counts + (nbr_second[:, k, None] == jnp.arange(width)[None, :]).astype(F32)
    mean_two = (jnp.dot(counts.astype(BF16), ext, preferred_element_type=F32) / FAN2).astype(BF16)
    layer_out = jnp.dot(hidden, w_second[0], preferred_element_type=F32)
    layer_out = (layer_out + jnp.dot(mean_two, w_second[1], preferred_element_type=F32)).astype(BF16)
    grad_terms = jnp.stack(
        [
            jnp.einsum("rh,ro->ho", hidden, cotangent, preferred_element_type=F32),
            jnp.einsum("rh,ro->ho", mean_two, cotangent, preferred_element_type=F32),
        ]
    )
    grad_second = lax.psum(grad_terms, AXES)
    d_self = jnp.einsum("ro,ho->rh", cotangent, w_second[0], preferred_element_type=F32)
    d_mean = jnp.einsum("ro,ho->rh", cotangent, w_second[1], preferred_element_type=F32) / FAN2
    d_ext = jnp.dot(counts.T, d_mean, precision=high)
    halo_grad = d_ext[OWN:].reshape(-1, slot_rows.shape[1], HID).astype(BF16)
    returned = lax.all_to_all(halo_grad, "graph", split_axis=0, concat_axis=0, tiled=True)
    onehot = (slot_rows.reshape(-1)[:, None] == jnp.arange(OWN)[None, :]).astype(BF16)
    d_back = jnp.einsum("sr,sh->rh", onehot, returned.reshape(-1, HID), preferred_element_type=F32)
    d_hidden = d_self + d_ext[:OWN] + d_back
    d_pre = (d_hidden * silu_grad(pre_one)).astype(BF16)
    piece = lax.all_gather(d_pre, "feat", axis=0, tiled=True)
    first_sum = jnp.einsum("rf,rh->fh", self_all, piece, preferred_element_type=F32)
    second_sum = jnp.einsum("rf,rh->fh", mean_all, piece, preferred_element_type=F32)
    grad_first = lax.psum(jnp.stack([first_sum, second_sum]), "graph")
    return (layer_out, grad_second, grad_first)


def solution(mesh):
    n_graph = mesh.shape["graph"]
    n_feat = mesh.shape["feat"]
    in_specs = (
        P("graph", "feat"),
        P(None, "feat", None),
        P(),
        P(AXES, None),
        P("graph", None),
        P(AXES, None, None),
        P(AXES, None),
    )
    out_specs = (P(AXES, None), P(), P(None, "feat", None))
    two = n_graph == 2 and n_feat == 16
    chosen = functools.partial(pair_body, n_feat) if two else body
    return jax.shard_map(chosen, mesh=mesh, in_specs=in_specs, out_specs=out_specs, check_vma=False)
```

```python
import functools

import jax
import jax.numpy as jnp
from jax import lax
from jax.experimental import pallas as pl
from jax.experimental.pallas import tpu as pltpu
from jax.sharding import PartitionSpec as P

HID = 256
FAN1 = 15
FAN2 = 10
OWN = 32
HALO = 8
LANES = 128
INTS = 16
F32 = jnp.float32
BF16 = jnp.bfloat16
AXES = ("graph", "feat")
PLANE = ((0, 0), (1, 1), (0, 1), (1, 0))


def silu_grad(value):
    sig = jax.nn.sigmoid(value)
    return sig * (1.0 + value * (1.0 - sig))


def dot(a, b, contract):
    return lax.dot_general(a, b, (contract, ((), ())), preferred_element_type=F32)


def write_pack(sends, cot, near, pack):
    my_z = lax.axis_index("feat") // 4
    for side in range(2):
        pack[side * OWN : (side + 1) * OWN, :] = cot[:, side * LANES : (side + 1) * LANES]
    lane = lax.broadcasted_iota(jnp.int32, (INTS, LANES), 1)
    row = lax.broadcasted_iota(jnp.int32, (INTS, LANES), 0)
    lists = jnp.concatenate([near[...], jnp.zeros((INTS - FAN2, OWN), jnp.int32)], axis=0)
    ints = jnp.where(lane // OWN == my_z, jnp.concatenate([lists] * (LANES // OWN), axis=1), 0)
    for g in range(2):
        for s in range(HALO):
            here = (row == FAN2) & (lane == my_z * OWN + g * HALO + s)
            ints = jnp.where(here, sends[0, g, s], ints)
    pack[2 * OWN : 2 * OWN + INTS, :] = ints.astype(F32).astype(BF16)


def first_kernel(
    feat_hbm, nbr_hbm, w_hbm, cot_hbm, near_hbm, sends_hbm, pack, x_t, kept, sent,
    feat_t, nbr_t, w_first, cot, near, sends, share, sems,
):
    pairs = ((nbr_hbm, nbr_t), (feat_hbm, feat_t), (w_hbm, w_first), (cot_hbm, cot), (near_hbm, near), (sends_hbm, sends))
    copies = [pltpu.make_async_copy(src, dst, sems.at[i]) for i, (src, dst) in enumerate(pairs)]
    for copy in copies:
        copy.start()
    copies[0].wait()
    sources = feat_t.shape[1]
    row = lax.broadcasted_iota(jnp.int32, (LANES, LANES), 0)
    for t in range(x_t.shape[0]):
        cols = slice(t * LANES, (t + 1) * LANES)
        low = nbr_t[:, cols] & (LANES - 1)
        unit = jnp.left_shift(1, 4 * jnp.right_shift(nbr_t[:, cols], 7))
        packed = jnp.zeros((LANES, LANES), jnp.int32)
        for k in range(FAN1):
            packed = packed + jnp.where(row == low[k : k + 1, :], unit[k : k + 1, :], 0)
        parts = [jnp.right_shift(packed, 4 * b) & 15 for b in range(sources // LANES)]
        counts = jnp.concatenate([part.astype(F32).astype(BF16) for part in parts], axis=0)
        if t == 0:
            copies[1].wait()
        mean = (dot(feat_t[...], counts, ((1,), (0,))) / FAN1).astype(BF16)
        chunk = jnp.concatenate([feat_t[:, cols], mean], axis=0)
        x_t[t] = chunk
        if t == 0:
            copies[2].wait()
        share[cols, :] = dot(chunk, w_first[...], ((0,), (0,)))
    line = x_t.shape[0]
    my_feat = lax.axis_index("feat")
    for c, out in enumerate((kept, sent)):
        for y in range(2):
            for z in range(line):
                owner = z * 4 + ((my_feat % 4) ^ (2 * y + c))
                block = share[pl.ds(pl.multiple_of(owner * OWN, OWN), OWN), :].astype(out.dtype)
                for side in range(2):
                    out[y * line + z, side * OWN : (side + 1) * OWN, :] = block[:, side * LANES : (side + 1) * LANES]
    for copy in copies[3:]:
        copy.wait()
    write_pack(sends, cot, near, pack)


def sum_core_kernel(mine, received, kept, sent):
    line = kept.shape[0]
    kept[...] = mine[0:line] + received[0:line].astype(F32)
    sent[...] = (mine[line : 2 * line] + received[line : 2 * line].astype(F32)).astype(BF16)


def sum_plane_kernel(pack, mine, received, message):
    total = (mine[...] + received[...].astype(F32)).astype(BF16)
    rows = total.shape[0] * total.shape[1]
    message[0:rows, :] = total.reshape(rows, LANES)
    message[rows:, :] = pack[...]


def sum_line_kernel(x_mine, x_peer, *refs):
    parts, (exact, message, slices) = refs[:-3], refs[-3:]
    my_z = lax.axis_index("feat") // 4
    line, width = exact.shape[0], exact.shape[1]
    rows = line * width
    sums = [part[0:rows, :].astype(F32) for part in parts]
    while len(sums) > 1:
        sums = [a + b for a, b in zip(sums[::2], sums[1::2])]
    total = sums[0].reshape(exact.shape)
    exact[...] = total
    total = total.astype(BF16)
    for z, part in enumerate(parts):
        message[2 * z * width : (2 * z + 1) * width, :] = total[z]
        at = pl.multiple_of((2 * (my_z ^ z) + 1) * width, width)
        message[pl.ds(at, width), :] = part[rows : rows + width, :]
    lists = [part[rows + width :, :].astype(F32) for part in parts]
    message[2 * rows :, :] = functools.reduce(lambda a, b: a + b, lists).astype(BF16)
    slices[0:line] = x_mine[...]
    slices[line : 2 * line] = x_peer[...]


def back_kernel(n_feat, plane_0, plane_1, plane_2, plane_3, w_second, cot_all, near_cot, d_hidden, own_counts, lists, spread, turn):
    line = n_feat // 4
    width = 2 * OWN
    my_graph = lax.axis_index("graph")
    my_z = lax.axis_index("feat") // 4
    my_y = lax.axis_index("feat") // 2 % 2
    for (x, y), message in zip(PLANE, (plane_0, plane_1, plane_2, plane_3)):
        at = (my_graph ^ x) * 2 + (my_y ^ y)
        lists[at] = message[2 * line * width :, :]
        for z in range(line):
            span = pl.ds(pl.multiple_of(at * LANES + z * OWN, OWN), OWN)
            for side in range(2):
                top = (2 * z + 1) * width + side * OWN
                cot_all[span, side * LANES : (side + 1) * LANES] = message[top : top + OWN, :]

    ints = lists[...].reshape(4 * INTS, LANES)
    source = lax.broadcasted_iota(jnp.int32, (LANES, LANES), 0)
    start = lax.broadcasted_iota(jnp.int32, (LANES, LANES), 1) // OWN * OWN
    pick = jnp.concatenate([jnp.where(source == start + s, 1.0, 0.0).astype(BF16) for s in range(2 * HALO)], axis=1)
    sent = dot(ints, pick, ((1,), (0,)))

    z_of = lax.broadcasted_iota(jnp.int32, (width, LANES), 1) // OWN
    slot_ix = lax.broadcasted_iota(jnp.int32, (width, LANES), 0).astype(F32)
    for y in range(2):
        total = jnp.zeros((line * width, HID), F32)
        for g in range(2):
            at = g * 2 + y
            entries = ints[at * INTS : (at + 1) * INTS, :].astype(F32)
            place_of = entries + float(g * OWN)
            for p in range(2):
                for s in range(HALO):
                    row = (p * 2 + y) * INTS + FAN2
                    there = sent[row : row + 1, (g * HALO + s) * LANES : (g * HALO + s + 1) * LANES] + p * OWN
                    place_of = jnp.where(entries == float(OWN + p * HALO + s), there, place_of)
            counts = jnp.zeros((width, LANES), F32)
            for k in range(FAN2):
                counts = counts + jnp.where(slot_ix == place_of[k : k + 1, :], 1.0, 0.0)
            spread[at] = counts
            block = jnp.concatenate([jnp.where(z_of == z, counts, 0.0) for z in range(line)], axis=0).astype(BF16)
            total = total + dot(block, cot_all[at * LANES : (at + 1) * LANES, :], ((1,), (0,)))
        total = (total / FAN2).astype(BF16)
        for z in range(line):
            for p in range(2):
                at = (p * 2 + y) * LANES + z * OWN
                near_cot[at : at + OWN, :] = total[z * width + p * OWN : z * width + (p + 1) * OWN, :]

    turn[...] = spread[pl.ds(my_graph * 2 + my_y, 1)][0].T
    own_counts[...] = turn[pl.ds(pl.multiple_of(my_z * OWN, OWN), OWN), :]

    part = dot(cot_all[...], w_second[0], ((1,), (1,)))
    d_hidden[...] = part + dot(near_cot[...], w_second[1], ((1,), (1,)))


def out_kernel(n_feat, mine, peer, exact, own_counts, w_second, layer_out, ext):
    my_graph = lax.axis_index("graph")
    my_z = lax.axis_index("feat") // 4
    own = exact[pl.ds(my_z, 1)][0]
    other = peer[pl.ds(pl.multiple_of(my_z * 4 * OWN, 4 * OWN), 2 * OWN), :].astype(F32)
    hiddens = []
    for value in (own, other):
        value = jnp.concatenate([value[0:OWN, :], value[OWN : 2 * OWN, :]], axis=1)
        hiddens.append((value * (0.5 + 0.5 * jnp.tanh(0.5 * value))).astype(BF16))
    ext[pl.ds(pl.multiple_of(my_graph * OWN, OWN), OWN), :] = hiddens[0]
    ext[pl.ds(pl.multiple_of((1 - my_graph) * OWN, OWN), OWN), :] = hiddens[1]
    mean = (dot(own_counts[...].astype(BF16), ext[...], ((1,), (0,))) / FAN2).astype(BF16)
    out = dot(hiddens[0], w_second[0], ((1,), (0,))) + dot(mean, w_second[1], ((1,), (0,)))
    layer_out[...] = out.astype(BF16)


def last_kernel(
    n_feat, plane_0, plane_1, plane_2, plane_3, cot, near_cot, d_hidden, x_mine, x_core,
    swapped, kept, hidden, d_pre, slices,
):
    my_graph = lax.axis_index("graph")
    my_feat = lax.axis_index("feat")
    rows = n_feat * OWN
    half = rows // 2
    line = n_feat // 4
    d_pre[...] = jnp.zeros_like(d_pre)
    my_y = my_feat // 2 % 2
    for (x, y), message in zip(PLANE, (plane_0, plane_1, plane_2, plane_3)):
        graph = my_graph ^ x
        for z in range(line):
            span = pl.ds(pl.multiple_of((graph * 2 + (my_y ^ y)) * LANES + z * OWN, OWN), OWN)
            top = 4 * z * OWN
            value = jnp.concatenate([message[top : top + OWN, :], message[top + OWN : top + 2 * OWN, :]], axis=1).astype(F32)
            sig = 0.5 + 0.5 * jnp.tanh(0.5 * value)
            hidden[span, :] = (value * sig).astype(BF16)
            slope = sig * (1.0 + value * (1.0 - sig))
            target = pl.ds(pl.multiple_of(graph * rows + (z * 4 + (my_feat % 4 ^ 2 * y)) * OWN, OWN), OWN)
            d_pre[target, :] = (d_hidden[span, :] * slope).astype(BF16)

    swapped[0:HID, :] = dot(hidden[...], cot[...], ((0,), (0,))).astype(BF16)
    swapped[HID : 2 * HID, :] = dot(hidden[...], near_cot[...], ((0,), (0,))).astype(BF16)

    for z in range(line):
        cols = slice(z * LANES, (z + 1) * LANES)
        for g in range(2):
            slices[g, 0 : 2 * OWN, cols] = x_mine[g * line + z]
            slices[g, 2 * OWN : 4 * OWN, cols] = x_core[g * line + z]
    mine = d_pre[pl.ds(pl.multiple_of(my_graph * rows, rows), rows), :]
    peer = d_pre[pl.ds(pl.multiple_of((1 - my_graph) * rows, rows), rows), :]
    first = dot(slices[0], mine, ((1,), (0,))) + dot(slices[1], peer, ((1,), (0,)))
    kept[...] = first[0 : 2 * OWN, :]
    swapped[2 * HID : 2 * HID + 2 * OWN, :] = first[2 * OWN : 4 * OWN, :].astype(BF16)


def add_kernel(mine, theirs, kept, grad_second, grad_first, second, first, sems):
    step = HID // 2
    copies = []
    for i in range(4):
        span = slice(i * step, (i + 1) * step)
        w, rows = i // 2, slice(i % 2 * step, (i % 2 + 1) * step)
        second[w, rows, :] = mine[span, :].astype(F32) + theirs[span, :].astype(F32)
        copies.append(pltpu.make_async_copy(second.at[w, rows, :], grad_second.at[w, rows, :], sems.at[i]))
        copies[-1].start()
    first[...] = kept[...] + theirs[2 * HID : 2 * HID + 2 * OWN, :].astype(F32)
    copies.append(pltpu.make_async_copy(first, grad_first, sems.at[4]))
    copies[-1].start()
    for copy in copies:
        copy.wait()


VMEM = pl.BlockSpec(memory_space=pltpu.VMEM)
ANY = pl.BlockSpec(memory_space=pl.ANY)
SMEM = pl.BlockSpec(memory_space=pltpu.SMEM)
LIMIT = 40 * 1024 * 1024


def call(kernel, outs, ins, scratch=(), name=None, place=VMEM):
    return pl.pallas_call(
        kernel,
        out_shape=[jax.ShapeDtypeStruct(shape, dtype) for shape, dtype in outs],
        in_specs=ins,
        out_specs=[place] * len(outs),
        scratch_shapes=list(scratch),
        compiler_params=pltpu.CompilerParams(vmem_limit_bytes=LIMIT),
        name=name,
    )


def swap(n_feat, value, relative):
    return lax.ppermute(value, AXES, [(d, d ^ relative) for d in range(2 * n_feat)])


def pair_body(n_feat, features, w_first, w_second, cotangent, nbr_first, send_rows, nbr_second):
    devices = 2 * n_feat
    rows = n_feat * OWN
    width = 2 * OWN
    line = n_feat // 4
    from_hbm = [features.T, nbr_first.T, w_first.reshape(width, HID), cotangent, nbr_second.T, send_rows]
    block = (line, width, LANES)
    pack, x_mine, kept, sent = call(
        first_kernel,
        [((width + INTS, LANES), BF16), (block, BF16), ((2 * line, width, LANES), F32), ((2 * line, width, LANES), BF16)],
        [ANY] * 6,
        [pltpu.VMEM(x.shape, x.dtype) for x in from_hbm[:-1]]
        + [pltpu.SMEM(send_rows.shape, jnp.int32), pltpu.VMEM((rows, HID), F32), pltpu.SemaphoreType.DMA((6,))],
        name="first",
    )(*[pltpu.with_memory_space_constraint(x, pltpu.HBM) for x in from_hbm])
    kept, sent = call(sum_core_kernel, [(block, F32), (block, BF16)], [VMEM] * 2, name="sum_core")(kept, swap(n_feat, sent, 1))
    x_peer = swap(n_feat, x_mine, n_feat)
    (message,) = call(
        sum_plane_kernel,
        [((line * width + width + INTS, LANES), BF16)],
        [VMEM] * 3,
        name="sum_plane",
    )(pack, kept, swap(n_feat, sent, 2))
    exact, message, slices = call(
        sum_line_kernel,
        [(block, F32), ((2 * line * width + INTS, LANES), BF16), ((2 * line, width, LANES), BF16)],
        [VMEM] * (line + 2),
        name="sum_line",
    )(x_mine, x_peer, message, *[swap(n_feat, message, 4 * z) for z in range(1, line)])
    plane = [message] + [swap(n_feat, message, r) for r in (n_feat + 2, 2, n_feat)]

    half = (devices // 2) * OWN
    cot, near_cot, d_hidden, own_counts = call(
        functools.partial(back_kernel, n_feat),
        [((half, HID), BF16), ((half, HID), BF16), ((half, HID), F32), ((OWN, width), F32)],
        [VMEM] * 5,
        [
            pltpu.VMEM((4, INTS, LANES), BF16),
            pltpu.VMEM((4, width, LANES), F32),
            pltpu.VMEM((LANES, width), F32),
        ],
        name="back",
    )(*plane, w_second)

    swapped, kept = call(
        functools.partial(last_kernel, n_feat),
        [((2 * HID + width, HID), BF16), ((width, HID), F32)],
        [VMEM] * 9,
        [
            pltpu.VMEM((half, HID), BF16),
            pltpu.VMEM((2 * half, HID), BF16),
            pltpu.VMEM((2, 2 * width, rows), BF16),
        ],
        name="last",
    )(*plane, cot, near_cot, d_hidden, slices, swap(n_feat, slices, 1))
    (layer_out,) = call(
        functools.partial(out_kernel, n_feat),
        [((OWN, HID), BF16)],
        [VMEM] * 5,
        [pltpu.VMEM((width, HID), BF16)],
        name="out",
    )(message, plane[3], exact, own_counts, w_second)
    grad_second, grad_first = call(
        add_kernel,
        [((2, HID, HID), F32), ((width, HID), F32)],
        [VMEM] * 3,
        [pltpu.VMEM((2, HID, HID), F32), pltpu.VMEM((width, HID), F32), pltpu.SemaphoreType.DMA((5,))],
        name="add",
        place=ANY,
    )(swapped, swap(n_feat, swapped, 1), kept)
    return (layer_out, grad_second, grad_first.reshape(2, OWN, HID))


def body(features, w_first, w_second, cotangent, nbr_first, send_rows, nbr_second):
    high = lax.Precision.HIGHEST
    targets = nbr_first.shape[0]
    gathered = features[nbr_first].astype(F32)
    mean_all = (jnp.sum(gathered, axis=1) / FAN1).astype(BF16)
    self_all = features[:targets]
    term = jnp.dot(self_all, w_first[0], preferred_element_type=F32)
    pre_one = lax.psum_scatter(
        term + jnp.dot(mean_all, w_first[1], preferred_element_type=F32),
        "feat",
        scatter_dimension=0,
        tiled=True,
    )
    hidden = jax.nn.silu(pre_one).astype(BF16)
    slot_rows = send_rows[0]
    valid = (slot_rows >= 0)[..., None]
    picked = hidden[jnp.maximum(slot_rows, 0)]
    outgoing_rows = jnp.where(valid, picked, jnp.zeros_like(picked))
    received = lax.all_to_all(outgoing_rows, "graph", split_axis=0, concat_axis=0, tiled=True)
    ext = jnp.concatenate([hidden, received.reshape(-1, HID)], axis=0)
    width = ext.shape[0]
    counts = jnp.zeros((OWN, width), F32)
    for k in range(FAN2):
        counts = counts + (nbr_second[:, k, None] == jnp.arange(width)[None, :]).astype(F32)
    mean_two = (jnp.dot(counts.astype(BF16), ext, preferred_element_type=F32) / FAN2).astype(BF16)
    layer_out = jnp.dot(hidden, w_second[0], preferred_element_type=F32)
    layer_out = (layer_out + jnp.dot(mean_two, w_second[1], preferred_element_type=F32)).astype(BF16)
    grad_terms = jnp.stack(
        [
            jnp.einsum("rh,ro->ho", hidden, cotangent, preferred_element_type=F32),
            jnp.einsum("rh,ro->ho", mean_two, cotangent, preferred_element_type=F32),
        ]
    )
    grad_second = lax.psum(grad_terms, AXES)
    d_self = jnp.einsum("ro,ho->rh", cotangent, w_second[0], preferred_element_type=F32)
    d_mean = jnp.einsum("ro,ho->rh", cotangent, w_second[1], preferred_element_type=F32) / FAN2
    d_ext = jnp.dot(counts.T, d_mean, precision=high)
    halo_grad = d_ext[OWN:].reshape(-1, slot_rows.shape[1], HID).astype(BF16)
    returned = lax.all_to_all(halo_grad, "graph", split_axis=0, concat_axis=0, tiled=True)
    onehot = (slot_rows.reshape(-1)[:, None] == jnp.arange(OWN)[None, :]).astype(BF16)
    d_back = jnp.einsum("sr,sh->rh", onehot, returned.reshape(-1, HID), preferred_element_type=F32)
    d_hidden = d_self + d_ext[:OWN] + d_back
    d_pre = (d_hidden * silu_grad(pre_one)).astype(BF16)
    piece = lax.all_gather(d_pre, "feat", axis=0, tiled=True)
    first_sum = jnp.einsum("rf,rh->fh", self_all, piece, preferred_element_type=F32)
    second_sum = jnp.einsum("rf,rh->fh", mean_all, piece, preferred_element_type=F32)
    grad_first = lax.psum(jnp.stack([first_sum, second_sum]), "graph")
    return (layer_out, grad_second, grad_first)


def solution(mesh):
    n_graph = mesh.shape["graph"]
    n_feat = mesh.shape["feat"]
    in_specs = (
        P("graph", "feat"),
        P(None, "feat", None),
        P(),
        P(AXES, None),
        P("graph", None),
        P(AXES, None, None),
        P(AXES, None),
    )
    out_specs = (P(AXES, None), P(), P(None, "feat", None))
    two = n_graph == 2 and n_feat == 16
    chosen = functools.partial(pair_body, n_feat) if two else body
    return jax.shard_map(chosen, mesh=mesh, in_specs=in_specs, out_specs=out_specs, check_vma=False)
```

```python
import functools

import jax
import jax.numpy as jnp
from jax import lax
from jax.experimental import pallas as pl
from jax.experimental.pallas import tpu as pltpu
from jax.sharding import PartitionSpec as P

HID = 256
FAN1 = 15
FAN2 = 10
OWN = 32
HALO = 8
LANES = 128
INTS = 16
F32 = jnp.float32
BF16 = jnp.bfloat16
AXES = ("graph", "feat")
PLANE = ((0, 0), (1, 0), (0, 1), (1, 1))


def silu_grad(value):
    sig = jax.nn.sigmoid(value)
    return sig * (1.0 + value * (1.0 - sig))


def dot(a, b, contract):
    return lax.dot_general(a, b, (contract, ((), ())), preferred_element_type=F32)


def write_pack(sends, cot, near, pack):
    my_z = lax.axis_index("feat") // 4
    for side in range(2):
        pack[side * OWN : (side + 1) * OWN, :] = cot[:, side * LANES : (side + 1) * LANES]
    lane = lax.broadcasted_iota(jnp.int32, (INTS, LANES), 1)
    row = lax.broadcasted_iota(jnp.int32, (INTS, LANES), 0)
    lists = jnp.concatenate([near[...], jnp.zeros((INTS - FAN2, OWN), jnp.int32)], axis=0)
    ints = jnp.where(lane // OWN == my_z, jnp.concatenate([lists] * (LANES // OWN), axis=1), 0)
    for g in range(2):
        for s in range(HALO):
            here = (row == FAN2) & (lane == my_z * OWN + g * HALO + s)
            ints = jnp.where(here, sends[0, g, s], ints)
    pack[2 * OWN : 2 * OWN + INTS, :] = ints.astype(F32).astype(BF16)


def first_kernel(
    feat_hbm, nbr_hbm, w_hbm, cot_hbm, near_hbm, sends_hbm, pack, x_t, kept, sent,
    feat_t, nbr_t, w_first, cot, near, sends, share, sems,
):
    pairs = ((nbr_hbm, nbr_t), (feat_hbm, feat_t), (w_hbm, w_first), (cot_hbm, cot), (near_hbm, near), (sends_hbm, sends))
    copies = [pltpu.make_async_copy(src, dst, sems.at[i]) for i, (src, dst) in enumerate(pairs)]
    for copy in copies:
        copy.start()
    copies[0].wait()
    sources = feat_t.shape[1]
    row = lax.broadcasted_iota(jnp.int32, (LANES, LANES), 0)
    for t in range(x_t.shape[0]):
        cols = slice(t * LANES, (t + 1) * LANES)
        low = nbr_t[:, cols] & (LANES - 1)
        unit = jnp.left_shift(1, 4 * jnp.right_shift(nbr_t[:, cols], 7))
        packed = jnp.zeros((LANES, LANES), jnp.int32)
        for k in range(FAN1):
            packed = packed + jnp.where(row == low[k : k + 1, :], unit[k : k + 1, :], 0)
        parts = [jnp.right_shift(packed, 4 * b) & 15 for b in range(sources // LANES)]
        counts = jnp.concatenate([part.astype(F32).astype(BF16) for part in parts], axis=0)
        if t == 0:
            copies[1].wait()
        mean = (dot(feat_t[...], counts, ((1,), (0,))) / FAN1).astype(BF16)
        chunk = jnp.concatenate([feat_t[:, cols], mean], axis=0)
        x_t[t] = chunk
        sent[2 * x_t.shape[0] + t] = chunk
        if t == 0:
            copies[2].wait()
        share[cols, :] = dot(chunk, w_first[...], ((0,), (0,)))
    line = x_t.shape[0]
    my_feat = lax.axis_index("feat")
    for c, out in enumerate((kept, sent)):
        for y in range(2):
            for z in range(line):
                owner = z * 4 + ((my_feat % 4) ^ (2 * y + c))
                block = share[pl.ds(pl.multiple_of(owner * OWN, OWN), OWN), :].astype(out.dtype)
                for side in range(2):
                    out[y * line + z, side * OWN : (side + 1) * OWN, :] = block[:, side * LANES : (side + 1) * LANES]
    for copy in copies[3:]:
        copy.wait()
    write_pack(sends, cot, near, pack)


def sum_core_kernel(mine, received, kept, sent):
    line = kept.shape[0]
    kept[...] = mine[0:line] + received[0:line].astype(F32)
    sent[...] = (mine[line : 2 * line] + received[line : 2 * line].astype(F32)).astype(BF16)


def sum_plane_kernel(pack, mine, received, message):
    total = (mine[...] + received[...].astype(F32)).astype(BF16)
    rows = total.shape[0] * total.shape[1]
    message[0:rows, :] = total.reshape(rows, LANES)
    message[rows:, :] = pack[...]


def sum_line_kernel(after, *refs):
    parts, (exact, message) = refs[:-2], refs[-2:]
    my_z = lax.axis_index("feat") // 4
    line, width = exact.shape[0], exact.shape[1]
    rows = line * width
    sums = [part[0:rows, :].astype(F32) for part in parts]
    while len(sums) > 1:
        sums = [a + b for a, b in zip(sums[::2], sums[1::2])]
    total = sums[0].reshape(exact.shape)
    exact[...] = total
    total = total.astype(BF16)
    for z, part in enumerate(parts):
        message[2 * z * width : (2 * z + 1) * width, :] = total[z]
        at = pl.multiple_of((2 * (my_z ^ z) + 1) * width, width)
        message[pl.ds(at, width), :] = part[rows : rows + width, :]
    lists = [part[rows + width :, :].astype(F32) for part in parts]
    message[2 * rows :, :] = functools.reduce(lambda a, b: a + b, lists).astype(BF16)


def back_kernel(n_feat, plane_0, plane_1, plane_2, plane_3, w_second, cot_all, near_cot, d_hidden, own_counts, lists, spread, turn):
    line = n_feat // 4
    width = 2 * OWN
    my_graph = lax.axis_index("graph")
    my_z = lax.axis_index("feat") // 4
    my_y = lax.axis_index("feat") // 2 % 2
    for (x, y), message in zip(PLANE, (plane_0, plane_1, plane_2, plane_3)):
        at = (my_graph ^ x) * 2 + (my_y ^ y)
        lists[at] = message[2 * line * width :, :]
        for z in range(line):
            span = pl.ds(pl.multiple_of(at * LANES + z * OWN, OWN), OWN)
            for side in range(2):
                top = (2 * z + 1) * width + side * OWN
                cot_all[span, side * LANES : (side + 1) * LANES] = message[top : top + OWN, :]

    ints = lists[...].reshape(4 * INTS, LANES)
    source = lax.broadcasted_iota(jnp.int32, (LANES, LANES), 0)
    start = lax.broadcasted_iota(jnp.int32, (LANES, LANES), 1) // OWN * OWN
    pick = jnp.concatenate([jnp.where(source == start + s, 1.0, 0.0).astype(BF16) for s in range(2 * HALO)], axis=1)
    sent = dot(ints, pick, ((1,), (0,)))

    z_of = lax.broadcasted_iota(jnp.int32, (width, LANES), 1) // OWN
    slot_ix = lax.broadcasted_iota(jnp.int32, (width, LANES), 0).astype(F32)
    for y in range(2):
        total = jnp.zeros((line * width, HID), F32)
        for g in range(2):
            at = g * 2 + y
            entries = ints[at * INTS : (at + 1) * INTS, :].astype(F32)
            place_of = entries + float(g * OWN)
            for p in range(2):
                for s in range(HALO):
                    row = (p * 2 + y) * INTS + FAN2
                    there = sent[row : row + 1, (g * HALO + s) * LANES : (g * HALO + s + 1) * LANES] + p * OWN
                    place_of = jnp.where(entries == float(OWN + p * HALO + s), there, place_of)
            counts = jnp.zeros((width, LANES), F32)
            for k in range(FAN2):
                counts = counts + jnp.where(slot_ix == place_of[k : k + 1, :], 1.0, 0.0)
            spread[at] = counts
            block = jnp.concatenate([jnp.where(z_of == z, counts, 0.0) for z in range(line)], axis=0).astype(BF16)
            total = total + dot(block, cot_all[at * LANES : (at + 1) * LANES, :], ((1,), (0,)))
        total = (total / FAN2).astype(BF16)
        for z in range(line):
            for p in range(2):
                at = (p * 2 + y) * LANES + z * OWN
                near_cot[at : at + OWN, :] = total[z * width + p * OWN : z * width + (p + 1) * OWN, :]

    turn[...] = spread[pl.ds(my_graph * 2 + my_y, 1)][0].T
    own_counts[...] = turn[pl.ds(pl.multiple_of(my_z * OWN, OWN), OWN), :]

    part = dot(cot_all[...], w_second[0], ((1,), (1,)))
    d_hidden[...] = part + dot(near_cot[...], w_second[1], ((1,), (1,)))


def out_kernel(n_feat, mine, peer, exact, own_counts, w_second, layer_out, ext):
    my_graph = lax.axis_index("graph")
    my_z = lax.axis_index("feat") // 4
    own = exact[pl.ds(my_z, 1)][0]
    other = peer[pl.ds(pl.multiple_of(my_z * 4 * OWN, 4 * OWN), 2 * OWN), :].astype(F32)
    hiddens = []
    for value in (own, other):
        value = jnp.concatenate([value[0:OWN, :], value[OWN : 2 * OWN, :]], axis=1)
        hiddens.append((value * (0.5 + 0.5 * jnp.tanh(0.5 * value))).astype(BF16))
    ext[pl.ds(pl.multiple_of(my_graph * OWN, OWN), OWN), :] = hiddens[0]
    ext[pl.ds(pl.multiple_of((1 - my_graph) * OWN, OWN), OWN), :] = hiddens[1]
    mean = (dot(own_counts[...].astype(BF16), ext[...], ((1,), (0,))) / FAN2).astype(BF16)
    out = dot(hiddens[0], w_second[0], ((1,), (0,))) + dot(mean, w_second[1], ((1,), (0,)))
    layer_out[...] = out.astype(BF16)


def last_kernel(
    n_feat, plane_0, plane_1, plane_2, plane_3, cot, near_cot, d_hidden, x_mine, x_core, x_peer, x_last,
    swapped, kept, hidden, d_pre, slices,
):
    my_graph = lax.axis_index("graph")
    my_feat = lax.axis_index("feat")
    rows = n_feat * OWN
    half = rows // 2
    line = n_feat // 4
    d_pre[...] = jnp.zeros_like(d_pre)
    my_y = my_feat // 2 % 2
    for (x, y), message in zip(PLANE, (plane_0, plane_1, plane_2, plane_3)):
        graph = my_graph ^ x
        for z in range(line):
            span = pl.ds(pl.multiple_of((graph * 2 + (my_y ^ y)) * LANES + z * OWN, OWN), OWN)
            top = 4 * z * OWN
            value = jnp.concatenate([message[top : top + OWN, :], message[top + OWN : top + 2 * OWN, :]], axis=1).astype(F32)
            sig = 0.5 + 0.5 * jnp.tanh(0.5 * value)
            hidden[span, :] = (value * sig).astype(BF16)
            slope = sig * (1.0 + value * (1.0 - sig))
            target = pl.ds(pl.multiple_of(graph * rows + (z * 4 + (my_feat % 4 ^ 2 * y)) * OWN, OWN), OWN)
            d_pre[target, :] = (d_hidden[span, :] * slope).astype(BF16)

    swapped[0:HID, :] = dot(hidden[...], cot[...], ((0,), (0,))).astype(BF16)
    swapped[HID : 2 * HID, :] = dot(hidden[...], near_cot[...], ((0,), (0,))).astype(BF16)

    for z in range(line):
        cols = slice(z * LANES, (z + 1) * LANES)
        slices[0, 0 : 2 * OWN, cols] = x_mine[z]
        slices[0, 2 * OWN : 4 * OWN, cols] = x_core[2 * line + z]
        slices[1, 0 : 2 * OWN, cols] = x_peer[z]
        slices[1, 2 * OWN : 4 * OWN, cols] = x_last[z]
    mine = d_pre[pl.ds(pl.multiple_of(my_graph * rows, rows), rows), :]
    peer = d_pre[pl.ds(pl.multiple_of((1 - my_graph) * rows, rows), rows), :]
    first = dot(slices[0], mine, ((1,), (0,))) + dot(slices[1], peer, ((1,), (0,)))
    kept[...] = first[0 : 2 * OWN, :]
    swapped[2 * HID : 2 * HID + 2 * OWN, :] = first[2 * OWN : 4 * OWN, :].astype(BF16)


def add_kernel(mine, theirs, kept, grad_second, grad_first):
    for w in range(2):
        span = slice(w * HID, (w + 1) * HID)
        grad_second[w] = mine[span, :].astype(F32) + theirs[span, :].astype(F32)
    grad_first[...] = kept[...] + theirs[2 * HID : 2 * HID + 2 * OWN, :].astype(F32)


VMEM = pl.BlockSpec(memory_space=pltpu.VMEM)
ANY = pl.BlockSpec(memory_space=pl.ANY)
SMEM = pl.BlockSpec(memory_space=pltpu.SMEM)
LIMIT = 40 * 1024 * 1024


def call(kernel, outs, ins, scratch=(), name=None, aliases=None):
    return pl.pallas_call(
        kernel,
        out_shape=[jax.ShapeDtypeStruct(shape, dtype) for shape, dtype in outs],
        in_specs=ins,
        out_specs=[VMEM] * len(outs),
        scratch_shapes=list(scratch),
        input_output_aliases=aliases or {},
        compiler_params=pltpu.CompilerParams(vmem_limit_bytes=LIMIT),
        name=name,
    )


def swap(n_feat, value, relative):
    return lax.ppermute(value, AXES, [(d, d ^ relative) for d in range(2 * n_feat)])


def pair_body(n_feat, features, w_first, w_second, cotangent, nbr_first, send_rows, nbr_second):
    devices = 2 * n_feat
    rows = n_feat * OWN
    width = 2 * OWN
    line = n_feat // 4
    from_hbm = [features.T, nbr_first.T, w_first.reshape(width, HID), cotangent, nbr_second.T, send_rows]
    block = (line, width, LANES)
    pack, x_mine, kept, sent = call(
        first_kernel,
        [((width + INTS, LANES), BF16), (block, BF16), ((2 * line, width, LANES), F32), ((3 * line, width, LANES), BF16)],
        [ANY] * 6,
        [pltpu.VMEM(x.shape, x.dtype) for x in from_hbm[:-1]]
        + [pltpu.SMEM(send_rows.shape, jnp.int32), pltpu.VMEM((rows, HID), F32), pltpu.SemaphoreType.DMA((6,))],
        name="first",
    )(*[pltpu.with_memory_space_constraint(x, pltpu.HBM) for x in from_hbm])
    x_core = swap(n_feat, sent, 1)
    kept, sent = call(sum_core_kernel, [(block, F32), (block, BF16)], [VMEM] * 2, name="sum_core")(kept, x_core)
    x_peer = swap(n_feat, x_mine, n_feat)
    (message,) = call(
        sum_plane_kernel,
        [((line * width + width + INTS, LANES), BF16)],
        [VMEM] * 3,
        name="sum_plane",
    )(pack, kept, swap(n_feat, sent, 2))
    x_last = swap(n_feat, x_peer, 1)
    exact, message = call(
        sum_line_kernel,
        [(block, F32), ((2 * line * width + INTS, LANES), BF16)],
        [ANY] + [VMEM] * line,
        name="sum_line",
    )(x_peer, message, *[swap(n_feat, message, 4 * z) for z in range(1, line)])
    plane = [swap(n_feat, message, r) for r in (n_feat + 2, 2, n_feat)]
    plane = [message, *plane[::-1]]

    half = (devices // 2) * OWN
    cot, near_cot, d_hidden, own_counts = call(
        functools.partial(back_kernel, n_feat),
        [((half, HID), BF16), ((half, HID), BF16), ((half, HID), F32), ((OWN, width), F32)],
        [VMEM] * 5,
        [
            pltpu.VMEM((4, INTS, LANES), BF16),
            pltpu.VMEM((4, width, LANES), F32),
            pltpu.VMEM((LANES, width), F32),
        ],
        name="back",
    )(*plane, w_second)

    swapped, kept = call(
        functools.partial(last_kernel, n_feat),
        [((2 * HID + width, HID), BF16), ((width, HID), F32)],
        [VMEM] * 11,
        [
            pltpu.VMEM((half, HID), BF16),
            pltpu.VMEM((2 * half, HID), BF16),
            pltpu.VMEM((2, 2 * width, rows), BF16),
        ],
        name="last",
    )(*plane, cot, near_cot, d_hidden, x_mine, x_core, x_peer, x_last)
    (layer_out,) = call(
        functools.partial(out_kernel, n_feat),
        [((OWN, HID), BF16)],
        [VMEM] * 5,
        [pltpu.VMEM((width, HID), BF16)],
        name="out",
    )(message, plane[1], exact, own_counts, w_second)
    grad_second, grad_first = call(
        add_kernel,
        [((2, HID, HID), F32), ((width, HID), F32)],
        [VMEM] * 3,
        name="add",
    )(swapped, swap(n_feat, swapped, 1), kept)
    return (layer_out, grad_second, grad_first.reshape(2, OWN, HID))


def body(features, w_first, w_second, cotangent, nbr_first, send_rows, nbr_second):
    high = lax.Precision.HIGHEST
    targets = nbr_first.shape[0]
    gathered = features[nbr_first].astype(F32)
    mean_all = (jnp.sum(gathered, axis=1) / FAN1).astype(BF16)
    self_all = features[:targets]
    term = jnp.dot(self_all, w_first[0], preferred_element_type=F32)
    pre_one = lax.psum_scatter(
        term + jnp.dot(mean_all, w_first[1], preferred_element_type=F32),
        "feat",
        scatter_dimension=0,
        tiled=True,
    )
    hidden = jax.nn.silu(pre_one).astype(BF16)
    slot_rows = send_rows[0]
    valid = (slot_rows >= 0)[..., None]
    picked = hidden[jnp.maximum(slot_rows, 0)]
    outgoing_rows = jnp.where(valid, picked, jnp.zeros_like(picked))
    received = lax.all_to_all(outgoing_rows, "graph", split_axis=0, concat_axis=0, tiled=True)
    ext = jnp.concatenate([hidden, received.reshape(-1, HID)], axis=0)
    width = ext.shape[0]
    counts = jnp.zeros((OWN, width), F32)
    for k in range(FAN2):
        counts = counts + (nbr_second[:, k, None] == jnp.arange(width)[None, :]).astype(F32)
    mean_two = (jnp.dot(counts.astype(BF16), ext, preferred_element_type=F32) / FAN2).astype(BF16)
    layer_out = jnp.dot(hidden, w_second[0], preferred_element_type=F32)
    layer_out = (layer_out + jnp.dot(mean_two, w_second[1], preferred_element_type=F32)).astype(BF16)
    grad_terms = jnp.stack(
        [
            jnp.einsum("rh,ro->ho", hidden, cotangent, preferred_element_type=F32),
            jnp.einsum("rh,ro->ho", mean_two, cotangent, preferred_element_type=F32),
        ]
    )
    grad_second = lax.psum(grad_terms, AXES)
    d_self = jnp.einsum("ro,ho->rh", cotangent, w_second[0], preferred_element_type=F32)
    d_mean = jnp.einsum("ro,ho->rh", cotangent, w_second[1], preferred_element_type=F32) / FAN2
    d_ext = jnp.dot(counts.T, d_mean, precision=high)
    halo_grad = d_ext[OWN:].reshape(-1, slot_rows.shape[1], HID).astype(BF16)
    returned = lax.all_to_all(halo_grad, "graph", split_axis=0, concat_axis=0, tiled=True)
    onehot = (slot_rows.reshape(-1)[:, None] == jnp.arange(OWN)[None, :]).astype(BF16)
    d_back = jnp.einsum("sr,sh->rh", onehot, returned.reshape(-1, HID), preferred_element_type=F32)
    d_hidden = d_self + d_ext[:OWN] + d_back
    d_pre = (d_hidden * silu_grad(pre_one)).astype(BF16)
    piece = lax.all_gather(d_pre, "feat", axis=0, tiled=True)
    first_sum = jnp.einsum("rf,rh->fh", self_all, piece, preferred_element_type=F32)
    second_sum = jnp.einsum("rf,rh->fh", mean_all, piece, preferred_element_type=F32)
    grad_first = lax.psum(jnp.stack([first_sum, second_sum]), "graph")
    return (layer_out, grad_second, grad_first)


def solution(mesh):
    n_graph = mesh.shape["graph"]
    n_feat = mesh.shape["feat"]
    in_specs = (
        P("graph", "feat"),
        P(None, "feat", None),
        P(),
        P(AXES, None),
        P("graph", None),
        P(AXES, None, None),
        P(AXES, None),
    )
    out_specs = (P(AXES, None), P(), P(None, "feat", None))
    two = n_graph == 2 and n_feat == 16
    chosen = functools.partial(pair_body, n_feat) if two else body
    return jax.shard_map(chosen, mesh=mesh, in_specs=in_specs, out_specs=out_specs, check_vma=False)
```

```python
import functools

import jax
import jax.numpy as jnp
from jax import lax
from jax.experimental import pallas as pl
from jax.experimental.pallas import tpu as pltpu
from jax.sharding import PartitionSpec as P

HID = 256
FAN1 = 15
FAN2 = 10
OWN = 32
HALO = 8
LANES = 128
INTS = 16
F32 = jnp.float32
BF16 = jnp.bfloat16
AXES = ("graph", "feat")
PLANE = ((0, 0), (1, 0), (0, 1), (1, 1))


def silu_grad(value):
    sig = jax.nn.sigmoid(value)
    return sig * (1.0 + value * (1.0 - sig))


def dot(a, b, contract):
    return lax.dot_general(a, b, (contract, ((), ())), preferred_element_type=F32)


def write_pack(sends, cot, near, pack):
    my_z = lax.axis_index("feat") // 4
    for side in range(2):
        pack[side * OWN : (side + 1) * OWN, :] = cot[:, side * LANES : (side + 1) * LANES]
    lane = lax.broadcasted_iota(jnp.int32, (INTS, LANES), 1)
    row = lax.broadcasted_iota(jnp.int32, (INTS, LANES), 0)
    lists = jnp.concatenate([near[...], jnp.zeros((INTS - FAN2, OWN), jnp.int32)], axis=0)
    ints = jnp.where(lane // OWN == my_z, jnp.concatenate([lists] * (LANES // OWN), axis=1), 0)
    for g in range(2):
        for s in range(HALO):
            here = (row == FAN2) & (lane == my_z * OWN + g * HALO + s)
            ints = jnp.where(here, sends[0, g, s], ints)
    pack[2 * OWN : 2 * OWN + INTS, :] = ints.astype(F32).astype(BF16)


def first_kernel(
    feat_hbm, nbr_hbm, w_hbm, cot_hbm, near_hbm, sends_hbm, pack, x_t, kept, sent,
    feat_t, nbr_t, w_first, cot, near, sends, share, sems,
):
    pairs = ((nbr_hbm, nbr_t), (feat_hbm, feat_t), (w_hbm, w_first), (cot_hbm, cot), (near_hbm, near), (sends_hbm, sends))
    copies = [pltpu.make_async_copy(src, dst, sems.at[i]) for i, (src, dst) in enumerate(pairs)]
    for copy in copies:
        copy.start()
    copies[0].wait()
    sources = feat_t.shape[1]
    row = lax.broadcasted_iota(jnp.int32, (LANES, LANES), 0)
    for t in range(x_t.shape[0]):
        cols = slice(t * LANES, (t + 1) * LANES)
        low = nbr_t[:, cols] & (LANES - 1)
        unit = jnp.left_shift(1, 4 * jnp.right_shift(nbr_t[:, cols], 7))
        packed = jnp.zeros((LANES, LANES), jnp.int32)
        for k in range(FAN1):
            packed = packed + jnp.where(row == low[k : k + 1, :], unit[k : k + 1, :], 0)
        parts = [jnp.right_shift(packed, 4 * b) & 15 for b in range(sources // LANES)]
        counts = jnp.concatenate([part.astype(F32).astype(BF16) for part in parts], axis=0)
        if t == 0:
            copies[1].wait()
        mean = (dot(feat_t[...], counts, ((1,), (0,))) / FAN1).astype(BF16)
        chunk = jnp.concatenate([feat_t[:, cols], mean], axis=0)
        x_t[t] = chunk
        sent[2 * x_t.shape[0] + t] = chunk
        if t == 0:
            copies[2].wait()
        share[cols, :] = dot(chunk, w_first[...], ((0,), (0,)))
    line = x_t.shape[0]
    my_feat = lax.axis_index("feat")
    for c, out in enumerate((kept, sent)):
        for y in range(2):
            for z in range(line):
                owner = z * 4 + ((my_feat % 4) ^ (2 * y + c))
                block = share[pl.ds(pl.multiple_of(owner * OWN, OWN), OWN), :].astype(out.dtype)
                for side in range(2):
                    out[y * line + z, side * OWN : (side + 1) * OWN, :] = block[:, side * LANES : (side + 1) * LANES]
    for copy in copies[3:]:
        copy.wait()
    write_pack(sends, cot, near, pack)


def sum_core_kernel(mine, received, kept, sent):
    line = kept.shape[0]
    kept[...] = mine[0:line] + received[0:line].astype(F32)
    sent[...] = (mine[line : 2 * line] + received[line : 2 * line].astype(F32)).astype(BF16)


def sum_plane_kernel(pack, mine, received, message):
    total = (mine[...] + received[...].astype(F32)).astype(BF16)
    rows = total.shape[0] * total.shape[1]
    message[0:rows, :] = total.reshape(rows, LANES)
    message[rows:, :] = pack[...]


def sum_line_kernel(after, *refs):
    parts, (exact, message) = refs[:-2], refs[-2:]
    my_z = lax.axis_index("feat") // 4
    line, width = exact.shape[0], exact.shape[1]
    rows = line * width
    parts = parts[:1] + parts[:0:-1]
    sums = [part[0:rows, :].astype(F32) for part in parts]
    while len(sums) > 1:
        sums = [a + b for a, b in zip(sums[::2], sums[1::2])]
    total = sums[0].reshape(exact.shape)
    exact[...] = total
    total = total.astype(BF16)
    for z, part in enumerate(parts):
        message[2 * z * width : (2 * z + 1) * width, :] = total[z]
        at = pl.multiple_of((2 * (my_z ^ z) + 1) * width, width)
        message[pl.ds(at, width), :] = part[rows : rows + width, :]
    lists = [part[rows + width :, :].astype(F32) for part in parts]
    message[2 * rows :, :] = functools.reduce(lambda a, b: a + b, lists).astype(BF16)


def back_kernel(n_feat, plane_0, plane_1, plane_2, plane_3, w_second, cot_all, near_cot, d_hidden, own_counts, lists, spread, turn):
    line = n_feat // 4
    width = 2 * OWN
    my_graph = lax.axis_index("graph")
    my_z = lax.axis_index("feat") // 4
    my_y = lax.axis_index("feat") // 2 % 2
    for (x, y), message in zip(PLANE, (plane_0, plane_1, plane_2, plane_3)):
        at = (my_graph ^ x) * 2 + (my_y ^ y)
        lists[at] = message[2 * line * width :, :]
        for z in range(line):
            span = pl.ds(pl.multiple_of(at * LANES + z * OWN, OWN), OWN)
            for side in range(2):
                top = (2 * z + 1) * width + side * OWN
                cot_all[span, side * LANES : (side + 1) * LANES] = message[top : top + OWN, :]

    ints = lists[...].reshape(4 * INTS, LANES)
    source = lax.broadcasted_iota(jnp.int32, (LANES, LANES), 0)
    start = lax.broadcasted_iota(jnp.int32, (LANES, LANES), 1) // OWN * OWN
    pick = jnp.concatenate([jnp.where(source == start + s, 1.0, 0.0).astype(BF16) for s in range(2 * HALO)], axis=1)
    sent = dot(ints, pick, ((1,), (0,)))

    z_of = lax.broadcasted_iota(jnp.int32, (width, LANES), 1) // OWN
    slot_ix = lax.broadcasted_iota(jnp.int32, (width, LANES), 0).astype(F32)
    for y in range(2):
        total = jnp.zeros((line * width, HID), F32)
        for g in range(2):
            at = g * 2 + y
            entries = ints[at * INTS : (at + 1) * INTS, :].astype(F32)
            place_of = entries + float(g * OWN)
            for p in range(2):
                for s in range(HALO):
                    row = (p * 2 + y) * INTS + FAN2
                    there = sent[row : row + 1, (g * HALO + s) * LANES : (g * HALO + s + 1) * LANES] + p * OWN
                    place_of = jnp.where(entries == float(OWN + p * HALO + s), there, place_of)
            counts = jnp.zeros((width, LANES), F32)
            for k in range(FAN2):
                counts = counts + jnp.where(slot_ix == place_of[k : k + 1, :], 1.0, 0.0)
            spread[at] = counts
            block = jnp.concatenate([jnp.where(z_of == z, counts, 0.0) for z in range(line)], axis=0).astype(BF16)
            total = total + dot(block, cot_all[at * LANES : (at + 1) * LANES, :], ((1,), (0,)))
        total = (total / FAN2).astype(BF16)
        for z in range(line):
            for p in range(2):
                at = (p * 2 + y) * LANES + z * OWN
                near_cot[at : at + OWN, :] = total[z * width + p * OWN : z * width + (p + 1) * OWN, :]

    turn[...] = spread[pl.ds(my_graph * 2 + my_y, 1)][0].T
    own_counts[...] = turn[pl.ds(pl.multiple_of(my_z * OWN, OWN), OWN), :]

    part = dot(cot_all[...], w_second[0], ((1,), (1,)))
    d_hidden[...] = part + dot(near_cot[...], w_second[1], ((1,), (1,)))


def out_kernel(n_feat, mine, peer, exact, own_counts, w_second, layer_out, ext):
    my_graph = lax.axis_index("graph")
    my_z = lax.axis_index("feat") // 4
    own = exact[pl.ds(my_z, 1)][0]
    other = peer[pl.ds(pl.multiple_of(my_z * 4 * OWN, 4 * OWN), 2 * OWN), :].astype(F32)
    hiddens = []
    for value in (own, other):
        value = jnp.concatenate([value[0:OWN, :], value[OWN : 2 * OWN, :]], axis=1)
        hiddens.append((value * (0.5 + 0.5 * jnp.tanh(0.5 * value))).astype(BF16))
    ext[pl.ds(pl.multiple_of(my_graph * OWN, OWN), OWN), :] = hiddens[0]
    ext[pl.ds(pl.multiple_of((1 - my_graph) * OWN, OWN), OWN), :] = hiddens[1]
    mean = (dot(own_counts[...].astype(BF16), ext[...], ((1,), (0,))) / FAN2).astype(BF16)
    out = dot(hiddens[0], w_second[0], ((1,), (0,))) + dot(mean, w_second[1], ((1,), (0,)))
    layer_out[...] = out.astype(BF16)


def last_kernel(
    n_feat, plane_0, plane_1, plane_2, plane_3, cot, near_cot, d_hidden, x_mine, x_core, x_peer, x_last,
    swapped, kept, hidden, d_pre, slices,
):
    my_graph = lax.axis_index("graph")
    my_feat = lax.axis_index("feat")
    rows = n_feat * OWN
    half = rows // 2
    line = n_feat // 4
    d_pre[...] = jnp.zeros_like(d_pre)
    my_y = my_feat // 2 % 2
    for (x, y), message in zip(PLANE, (plane_0, plane_1, plane_2, plane_3)):
        graph = my_graph ^ x
        for z in range(line):
            span = pl.ds(pl.multiple_of((graph * 2 + (my_y ^ y)) * LANES + z * OWN, OWN), OWN)
            top = 4 * z * OWN
            value = jnp.concatenate([message[top : top + OWN, :], message[top + OWN : top + 2 * OWN, :]], axis=1).astype(F32)
            sig = 0.5 + 0.5 * jnp.tanh(0.5 * value)
            hidden[span, :] = (value * sig).astype(BF16)
            slope = sig * (1.0 + value * (1.0 - sig))
            target = pl.ds(pl.multiple_of(graph * rows + (z * 4 + (my_feat % 4 ^ 2 * y)) * OWN, OWN), OWN)
            d_pre[target, :] = (d_hidden[span, :] * slope).astype(BF16)

    swapped[0:HID, :] = dot(hidden[...], cot[...], ((0,), (0,))).astype(BF16)
    swapped[HID : 2 * HID, :] = dot(hidden[...], near_cot[...], ((0,), (0,))).astype(BF16)

    for z in range(line):
        cols = slice(z * LANES, (z + 1) * LANES)
        slices[0, 0 : 2 * OWN, cols] = x_mine[z]
        slices[0, 2 * OWN : 4 * OWN, cols] = x_core[2 * line + z]
        slices[1, 0 : 2 * OWN, cols] = x_peer[z]
        slices[1, 2 * OWN : 4 * OWN, cols] = x_last[z]
    mine = d_pre[pl.ds(pl.multiple_of(my_graph * rows, rows), rows), :]
    peer = d_pre[pl.ds(pl.multiple_of((1 - my_graph) * rows, rows), rows), :]
    first = dot(slices[0], mine, ((1,), (0,))) + dot(slices[1], peer, ((1,), (0,)))
    kept[...] = first[0 : 2 * OWN, :]
    swapped[2 * HID : 2 * HID + 2 * OWN, :] = first[2 * OWN : 4 * OWN, :].astype(BF16)


def add_kernel(mine, theirs, kept, grad_second, grad_first):
    for w in range(2):
        span = slice(w * HID, (w + 1) * HID)
        grad_second[w] = mine[span, :].astype(F32) + theirs[span, :].astype(F32)
    grad_first[...] = kept[...] + theirs[2 * HID : 2 * HID + 2 * OWN, :].astype(F32)


VMEM = pl.BlockSpec(memory_space=pltpu.VMEM)
ANY = pl.BlockSpec(memory_space=pl.ANY)
SMEM = pl.BlockSpec(memory_space=pltpu.SMEM)
LIMIT = 40 * 1024 * 1024


def call(kernel, outs, ins, scratch=(), name=None, aliases=None):
    return pl.pallas_call(
        kernel,
        out_shape=[jax.ShapeDtypeStruct(shape, dtype) for shape, dtype in outs],
        in_specs=ins,
        out_specs=[VMEM] * len(outs),
        scratch_shapes=list(scratch),
        input_output_aliases=aliases or {},
        compiler_params=pltpu.CompilerParams(vmem_limit_bytes=LIMIT),
        name=name,
    )


def swap(n_feat, value, relative):
    return lax.ppermute(value, AXES, [(d, d ^ relative) for d in range(2 * n_feat)])


def pair_body(n_feat, features, w_first, w_second, cotangent, nbr_first, send_rows, nbr_second):
    devices = 2 * n_feat
    rows = n_feat * OWN
    width = 2 * OWN
    line = n_feat // 4
    from_hbm = [features.T, nbr_first.T, w_first.reshape(width, HID), cotangent, nbr_second.T, send_rows]
    block = (line, width, LANES)
    pack, x_mine, kept, sent = call(
        first_kernel,
        [((width + INTS, LANES), BF16), (block, BF16), ((2 * line, width, LANES), F32), ((3 * line, width, LANES), BF16)],
        [ANY] * 6,
        [pltpu.VMEM(x.shape, x.dtype) for x in from_hbm[:-1]]
        + [pltpu.SMEM(send_rows.shape, jnp.int32), pltpu.VMEM((rows, HID), F32), pltpu.SemaphoreType.DMA((6,))],
        name="first",
    )(*[pltpu.with_memory_space_constraint(x, pltpu.HBM) for x in from_hbm])
    x_core = swap(n_feat, sent, 1)
    kept, sent = call(sum_core_kernel, [(block, F32), (block, BF16)], [VMEM] * 2, name="sum_core")(kept, x_core)
    x_peer = swap(n_feat, x_mine, n_feat)
    (message,) = call(
        sum_plane_kernel,
        [((line * width + width + INTS, LANES), BF16)],
        [VMEM] * 3,
        name="sum_plane",
    )(pack, kept, swap(n_feat, sent, 2))
    x_last = swap(n_feat, x_peer, 1)
    exact, message = call(
        sum_line_kernel,
        [(block, F32), ((2 * line * width + INTS, LANES), BF16)],
        [ANY] + [VMEM] * line,
        name="sum_line",
    )(x_peer, message, *[swap(n_feat, message, 4 * z) for z in range(line - 1, 0, -1)])
    plane = [swap(n_feat, message, r) for r in (n_feat + 2, 2, n_feat)]
    plane = [message, *plane[::-1]]

    half = (devices // 2) * OWN
    cot, near_cot, d_hidden, own_counts = call(
        functools.partial(back_kernel, n_feat),
        [((half, HID), BF16), ((half, HID), BF16), ((half, HID), F32), ((OWN, width), F32)],
        [VMEM] * 5,
        [
            pltpu.VMEM((4, INTS, LANES), BF16),
            pltpu.VMEM((4, width, LANES), F32),
            pltpu.VMEM((LANES, width), F32),
        ],
        name="back",
    )(*plane, w_second)

    swapped, kept = call(
        functools.partial(last_kernel, n_feat),
        [((2 * HID + width, HID), BF16), ((width, HID), F32)],
        [VMEM] * 11,
        [
            pltpu.VMEM((half, HID), BF16),
            pltpu.VMEM((2 * half, HID), BF16),
            pltpu.VMEM((2, 2 * width, rows), BF16),
        ],
        name="last",
    )(*plane, cot, near_cot, d_hidden, x_mine, x_core, x_peer, x_last)
    (layer_out,) = call(
        functools.partial(out_kernel, n_feat),
        [((OWN, HID), BF16)],
        [VMEM] * 5,
        [pltpu.VMEM((width, HID), BF16)],
        name="out",
    )(message, plane[1], exact, own_counts, w_second)
    grad_second, grad_first = call(
        add_kernel,
        [((2, HID, HID), F32), ((width, HID), F32)],
        [VMEM] * 3,
        name="add",
    )(swapped, swap(n_feat, swapped, 1), kept)
    return (layer_out, grad_second, grad_first.reshape(2, OWN, HID))


def body(features, w_first, w_second, cotangent, nbr_first, send_rows, nbr_second):
    high = lax.Precision.HIGHEST
    targets = nbr_first.shape[0]
    gathered = features[nbr_first].astype(F32)
    mean_all = (jnp.sum(gathered, axis=1) / FAN1).astype(BF16)
    self_all = features[:targets]
    term = jnp.dot(self_all, w_first[0], preferred_element_type=F32)
    pre_one = lax.psum_scatter(
        term + jnp.dot(mean_all, w_first[1], preferred_element_type=F32),
        "feat",
        scatter_dimension=0,
        tiled=True,
    )
    hidden = jax.nn.silu(pre_one).astype(BF16)
    slot_rows = send_rows[0]
    valid = (slot_rows >= 0)[..., None]
    picked = hidden[jnp.maximum(slot_rows, 0)]
    outgoing_rows = jnp.where(valid, picked, jnp.zeros_like(picked))
    received = lax.all_to_all(outgoing_rows, "graph", split_axis=0, concat_axis=0, tiled=True)
    ext = jnp.concatenate([hidden, received.reshape(-1, HID)], axis=0)
    width = ext.shape[0]
    counts = jnp.zeros((OWN, width), F32)
    for k in range(FAN2):
        counts = counts + (nbr_second[:, k, None] == jnp.arange(width)[None, :]).astype(F32)
    mean_two = (jnp.dot(counts.astype(BF16), ext, preferred_element_type=F32) / FAN2).astype(BF16)
    layer_out = jnp.dot(hidden, w_second[0], preferred_element_type=F32)
    layer_out = (layer_out + jnp.dot(mean_two, w_second[1], preferred_element_type=F32)).astype(BF16)
    grad_terms = jnp.stack(
        [
            jnp.einsum("rh,ro->ho", hidden, cotangent, preferred_element_type=F32),
            jnp.einsum("rh,ro->ho", mean_two, cotangent, preferred_element_type=F32),
        ]
    )
    grad_second = lax.psum(grad_terms, AXES)
    d_self = jnp.einsum("ro,ho->rh", cotangent, w_second[0], preferred_element_type=F32)
    d_mean = jnp.einsum("ro,ho->rh", cotangent, w_second[1], preferred_element_type=F32) / FAN2
    d_ext = jnp.dot(counts.T, d_mean, precision=high)
    halo_grad = d_ext[OWN:].reshape(-1, slot_rows.shape[1], HID).astype(BF16)
    returned = lax.all_to_all(halo_grad, "graph", split_axis=0, concat_axis=0, tiled=True)
    onehot = (slot_rows.reshape(-1)[:, None] == jnp.arange(OWN)[None, :]).astype(BF16)
    d_back = jnp.einsum("sr,sh->rh", onehot, returned.reshape(-1, HID), preferred_element_type=F32)
    d_hidden = d_self + d_ext[:OWN] + d_back
    d_pre = (d_hidden * silu_grad(pre_one)).astype(BF16)
    piece = lax.all_gather(d_pre, "feat", axis=0, tiled=True)
    first_sum = jnp.einsum("rf,rh->fh", self_all, piece, preferred_element_type=F32)
    second_sum = jnp.einsum("rf,rh->fh", mean_all, piece, preferred_element_type=F32)
    grad_first = lax.psum(jnp.stack([first_sum, second_sum]), "graph")
    return (layer_out, grad_second, grad_first)


def solution(mesh):
    n_graph = mesh.shape["graph"]
    n_feat = mesh.shape["feat"]
    in_specs = (
        P("graph", "feat"),
        P(None, "feat", None),
        P(),
        P(AXES, None),
        P("graph", None),
        P(AXES, None, None),
        P(AXES, None),
    )
    out_specs = (P(AXES, None), P(), P(None, "feat", None))
    two = n_graph == 2 and n_feat == 16
    chosen = functools.partial(pair_body, n_feat) if two else body
    return jax.shard_map(chosen, mesh=mesh, in_specs=in_specs, out_specs=out_specs, check_vma=False)
```

```python
import functools

import jax
import jax.numpy as jnp
from jax import lax
from jax.experimental import pallas as pl
from jax.experimental.pallas import tpu as pltpu
from jax.sharding import PartitionSpec as P

HID = 256
FAN1 = 15
FAN2 = 10
OWN = 32
HALO = 8
LANES = 128
INTS = 16
F32 = jnp.float32
BF16 = jnp.bfloat16
AXES = ("graph", "feat")
PLANE = ((0, 0), (1, 0), (0, 1), (1, 1))


def silu_grad(value):
    sig = jax.nn.sigmoid(value)
    return sig * (1.0 + value * (1.0 - sig))


def dot(a, b, contract):
    return lax.dot_general(a, b, (contract, ((), ())), preferred_element_type=F32)


def write_pack(sends, cot, near, pack):
    my_z = lax.axis_index("feat") // 4
    for side in range(2):
        pack[side * OWN : (side + 1) * OWN, :] = cot[:, side * LANES : (side + 1) * LANES]
    lane = lax.broadcasted_iota(jnp.int32, (INTS, LANES), 1)
    row = lax.broadcasted_iota(jnp.int32, (INTS, LANES), 0)
    lists = jnp.concatenate([near[...], jnp.zeros((INTS - FAN2, OWN), jnp.int32)], axis=0)
    ints = jnp.where(lane // OWN == my_z, jnp.concatenate([lists] * (LANES // OWN), axis=1), 0)
    for g in range(2):
        for s in range(HALO):
            here = (row == FAN2) & (lane == my_z * OWN + g * HALO + s)
            ints = jnp.where(here, sends[0, g, s], ints)
    pack[2 * OWN : 2 * OWN + INTS, :] = ints.astype(F32).astype(BF16)


def first_kernel(
    feat_hbm, nbr_hbm, w_hbm, cot_hbm, near_hbm, sends_hbm, pack, x_t, kept, sent,
    feat_t, nbr_t, w_first, cot, near, sends, share, sems,
):
    pairs = ((nbr_hbm, nbr_t), (feat_hbm, feat_t), (w_hbm, w_first), (cot_hbm, cot), (near_hbm, near), (sends_hbm, sends))
    copies = [pltpu.make_async_copy(src, dst, sems.at[i]) for i, (src, dst) in enumerate(pairs)]
    for copy in copies:
        copy.start()
    copies[0].wait()
    sources = feat_t.shape[1]
    row = lax.broadcasted_iota(jnp.int32, (LANES, LANES), 0)
    for t in range(x_t.shape[0]):
        cols = slice(t * LANES, (t + 1) * LANES)
        low = nbr_t[:, cols] & (LANES - 1)
        unit = jnp.left_shift(1, 4 * jnp.right_shift(nbr_t[:, cols], 7))
        packed = jnp.zeros((LANES, LANES), jnp.int32)
        for k in range(FAN1):
            packed = packed + jnp.where(row == low[k : k + 1, :], unit[k : k + 1, :], 0)
        parts = [jnp.right_shift(packed, 4 * b) & 15 for b in range(sources // LANES)]
        counts = jnp.concatenate([part.astype(F32).astype(BF16) for part in parts], axis=0)
        if t == 0:
            copies[1].wait()
        mean = (dot(feat_t[...], counts, ((1,), (0,))) / FAN1).astype(BF16)
        chunk = jnp.concatenate([feat_t[:, cols], mean], axis=0)
        x_t[t] = chunk
        sent[2 * x_t.shape[0] + t] = chunk
        if t == 0:
            copies[2].wait()
        share[cols, :] = dot(chunk, w_first[...], ((0,), (0,)))
    line = x_t.shape[0]
    my_feat = lax.axis_index("feat")
    for c, out in enumerate((kept, sent)):
        for y in range(2):
            for z in range(line):
                owner = z * 4 + ((my_feat % 4) ^ (2 * y + c))
                block = share[pl.ds(pl.multiple_of(owner * OWN, OWN), OWN), :].astype(out.dtype)
                for side in range(2):
                    out[y * line + z, side * OWN : (side + 1) * OWN, :] = block[:, side * LANES : (side + 1) * LANES]
    for copy in copies[3:]:
        copy.wait()
    write_pack(sends, cot, near, pack)


def sum_core_kernel(mine, received, kept, sent):
    line = kept.shape[0]
    kept[...] = mine[0:line] + received[0:line].astype(F32)
    sent[...] = (mine[line : 2 * line] + received[line : 2 * line].astype(F32)).astype(BF16)


def sum_plane_kernel(pack, mine, received, message):
    total = (mine[...] + received[...].astype(F32)).astype(BF16)
    rows = total.shape[0] * total.shape[1]
    message[0:rows, :] = total.reshape(rows, LANES)
    message[rows:, :] = pack[...]


def sum_line_kernel(after, *refs):
    parts, (exact, message) = refs[:-2], refs[-2:]
    my_z = lax.axis_index("feat") // 4
    line, width = exact.shape[0], exact.shape[1]
    rows = line * width
    sums = [part[0:rows, :].astype(F32) for part in parts]
    while len(sums) > 1:
        sums = [a + b for a, b in zip(sums[::2], sums[1::2])]
    total = sums[0].reshape(exact.shape)
    exact[...] = total
    total = total.astype(BF16)
    for z, part in enumerate(parts):
        message[2 * z * width : (2 * z + 1) * width, :] = total[z]
        at = pl.multiple_of((2 * (my_z ^ z) + 1) * width, width)
        message[pl.ds(at, width), :] = part[rows : rows + width, :]
    lists = [part[rows + width :, :].astype(F32) for part in parts]
    message[2 * rows :, :] = functools.reduce(lambda a, b: a + b, lists).astype(BF16)


def write_back(n_feat, plane_0, plane_1, plane_2, plane_3, w_second, cot_all, near_cot, d_hidden, own_counts, lists, spread, turn):
    line = n_feat // 4
    width = 2 * OWN
    my_graph = lax.axis_index("graph")
    my_z = lax.axis_index("feat") // 4
    my_y = lax.axis_index("feat") // 2 % 2
    for (x, y), message in zip(PLANE, (plane_0, plane_1, plane_2, plane_3)):
        at = (my_graph ^ x) * 2 + (my_y ^ y)
        lists[at] = message[2 * line * width :, :]
        for z in range(line):
            span = pl.ds(pl.multiple_of(at * LANES + z * OWN, OWN), OWN)
            for side in range(2):
                top = (2 * z + 1) * width + side * OWN
                cot_all[span, side * LANES : (side + 1) * LANES] = message[top : top + OWN, :]

    ints = lists[...].reshape(4 * INTS, LANES)
    source = lax.broadcasted_iota(jnp.int32, (LANES, LANES), 0)
    start = lax.broadcasted_iota(jnp.int32, (LANES, LANES), 1) // OWN * OWN
    pick = jnp.concatenate([jnp.where(source == start + s, 1.0, 0.0).astype(BF16) for s in range(2 * HALO)], axis=1)
    sent = dot(ints, pick, ((1,), (0,)))

    z_of = lax.broadcasted_iota(jnp.int32, (width, LANES), 1) // OWN
    slot_ix = lax.broadcasted_iota(jnp.int32, (width, LANES), 0).astype(F32)
    for y in range(2):
        total = jnp.zeros((line * width, HID), F32)
        for g in range(2):
            at = g * 2 + y
            entries = ints[at * INTS : (at + 1) * INTS, :].astype(F32)
            place_of = entries + float(g * OWN)
            for p in range(2):
                for s in range(HALO):
                    row = (p * 2 + y) * INTS + FAN2
                    there = sent[row : row + 1, (g * HALO + s) * LANES : (g * HALO + s + 1) * LANES] + p * OWN
                    place_of = jnp.where(entries == float(OWN + p * HALO + s), there, place_of)
            counts = jnp.zeros((width, LANES), F32)
            for k in range(FAN2):
                counts = counts + jnp.where(slot_ix == place_of[k : k + 1, :], 1.0, 0.0)
            spread[at] = counts
            block = jnp.concatenate([jnp.where(z_of == z, counts, 0.0) for z in range(line)], axis=0).astype(BF16)
            total = total + dot(block, cot_all[at * LANES : (at + 1) * LANES, :], ((1,), (0,)))
        total = (total / FAN2).astype(BF16)
        for z in range(line):
            for p in range(2):
                at = (p * 2 + y) * LANES + z * OWN
                near_cot[at : at + OWN, :] = total[z * width + p * OWN : z * width + (p + 1) * OWN, :]

    turn[...] = spread[pl.ds(my_graph * 2 + my_y, 1)][0].T
    own_counts[...] = turn[pl.ds(pl.multiple_of(my_z * OWN, OWN), OWN), :]

    part = dot(cot_all[...], w_second[0], ((1,), (1,)))
    d_hidden[...] = part + dot(near_cot[...], w_second[1], ((1,), (1,)))


def out_kernel(n_feat, peer, exact, own_counts, w_second, layer_out, ext):
    my_graph = lax.axis_index("graph")
    my_z = lax.axis_index("feat") // 4
    own = exact[pl.ds(my_z, 1)][0]
    far = peer[pl.ds(pl.multiple_of(my_z * 4 * OWN, 4 * OWN), 2 * OWN), :].astype(F32)
    hiddens = []
    for value in (own, far):
        value = jnp.concatenate([value[0:OWN, :], value[OWN : 2 * OWN, :]], axis=1)
        hiddens.append((value * (0.5 + 0.5 * jnp.tanh(0.5 * value))).astype(BF16))
    ext[pl.ds(pl.multiple_of(my_graph * OWN, OWN), OWN), :] = hiddens[0]
    ext[pl.ds(pl.multiple_of((1 - my_graph) * OWN, OWN), OWN), :] = hiddens[1]
    mean = (dot(own_counts[...].astype(BF16), ext[...], ((1,), (0,))) / FAN2).astype(BF16)
    out = dot(hiddens[0], w_second[0], ((1,), (0,))) + dot(mean, w_second[1], ((1,), (0,)))
    layer_out[...] = out.astype(BF16)


def last_kernel(
    n_feat, plane_0, plane_1, plane_2, plane_3, w_second, x_mine, x_core, x_peer, x_last,
    own_counts, swapped, kept, cot, near_cot, d_hidden, lists, spread, turn, hidden, d_pre, slices,
):
    write_back(n_feat, plane_0, plane_1, plane_2, plane_3, w_second, cot, near_cot, d_hidden, own_counts, lists, spread, turn)
    my_graph = lax.axis_index("graph")
    my_feat = lax.axis_index("feat")
    rows = n_feat * OWN
    half = rows // 2
    line = n_feat // 4
    d_pre[...] = jnp.zeros_like(d_pre)
    my_y = my_feat // 2 % 2
    for (x, y), message in zip(PLANE, (plane_0, plane_1, plane_2, plane_3)):
        graph = my_graph ^ x
        for z in range(line):
            span = pl.ds(pl.multiple_of((graph * 2 + (my_y ^ y)) * LANES + z * OWN, OWN), OWN)
            top = 4 * z * OWN
            value = jnp.concatenate([message[top : top + OWN, :], message[top + OWN : top + 2 * OWN, :]], axis=1).astype(F32)
            sig = 0.5 + 0.5 * jnp.tanh(0.5 * value)
            hidden[span, :] = (value * sig).astype(BF16)
            slope = sig * (1.0 + value * (1.0 - sig))
            target = pl.ds(pl.multiple_of(graph * rows + (z * 4 + (my_feat % 4 ^ 2 * y)) * OWN, OWN), OWN)
            d_pre[target, :] = (d_hidden[span, :] * slope).astype(BF16)

    swapped[0:HID, :] = dot(hidden[...], cot[...], ((0,), (0,))).astype(BF16)
    swapped[HID : 2 * HID, :] = dot(hidden[...], near_cot[...], ((0,), (0,))).astype(BF16)

    for z in range(line):
        cols = slice(z * LANES, (z + 1) * LANES)
        slices[0, 0 : 2 * OWN, cols] = x_mine[z]
        slices[0, 2 * OWN : 4 * OWN, cols] = x_core[2 * line + z]
        slices[1, 0 : 2 * OWN, cols] = x_peer[z]
        slices[1, 2 * OWN : 4 * OWN, cols] = x_last[z]
    mine = d_pre[pl.ds(pl.multiple_of(my_graph * rows, rows), rows), :]
    peer = d_pre[pl.ds(pl.multiple_of((1 - my_graph) * rows, rows), rows), :]
    first = dot(slices[0], mine, ((1,), (0,))) + dot(slices[1], peer, ((1,), (0,)))
    kept[...] = first[0 : 2 * OWN, :]
    swapped[2 * HID : 2 * HID + 2 * OWN, :] = first[2 * OWN : 4 * OWN, :].astype(BF16)


def add_kernel(mine, theirs, kept, grad_second, grad_first):
    for w in range(2):
        span = slice(w * HID, (w + 1) * HID)
        grad_second[w] = mine[span, :].astype(F32) + theirs[span, :].astype(F32)
    grad_first[...] = kept[...] + theirs[2 * HID : 2 * HID + 2 * OWN, :].astype(F32)


VMEM = pl.BlockSpec(memory_space=pltpu.VMEM)
ANY = pl.BlockSpec(memory_space=pl.ANY)
SMEM = pl.BlockSpec(memory_space=pltpu.SMEM)
LIMIT = 40 * 1024 * 1024


def call(kernel, outs, ins, scratch=(), name=None, aliases=None):
    return pl.pallas_call(
        kernel,
        out_shape=[jax.ShapeDtypeStruct(shape, dtype) for shape, dtype in outs],
        in_specs=ins,
        out_specs=[VMEM] * len(outs),
        scratch_shapes=list(scratch),
        input_output_aliases=aliases or {},
        compiler_params=pltpu.CompilerParams(vmem_limit_bytes=LIMIT),
        name=name,
    )


def swap(n_feat, value, relative):
    return lax.ppermute(value, AXES, [(d, d ^ relative) for d in range(2 * n_feat)])


def pair_body(n_feat, features, w_first, w_second, cotangent, nbr_first, send_rows, nbr_second):
    devices = 2 * n_feat
    rows = n_feat * OWN
    width = 2 * OWN
    line = n_feat // 4
    from_hbm = [features.T, nbr_first.T, w_first.reshape(width, HID), cotangent, nbr_second.T, send_rows]
    block = (line, width, LANES)
    pack, x_mine, kept, sent = call(
        first_kernel,
        [((width + INTS, LANES), BF16), (block, BF16), ((2 * line, width, LANES), F32), ((3 * line, width, LANES), BF16)],
        [ANY] * 6,
        [pltpu.VMEM(x.shape, x.dtype) for x in from_hbm[:-1]]
        + [pltpu.SMEM(send_rows.shape, jnp.int32), pltpu.VMEM((rows, HID), F32), pltpu.SemaphoreType.DMA((6,))],
        name="first",
    )(*[pltpu.with_memory_space_constraint(x, pltpu.HBM) for x in from_hbm])
    x_core = swap(n_feat, sent, 1)
    kept, sent = call(sum_core_kernel, [(block, F32), (block, BF16)], [VMEM] * 2, name="sum_core")(kept, x_core)
    x_peer = swap(n_feat, x_mine, n_feat)
    (message,) = call(
        sum_plane_kernel,
        [((line * width + width + INTS, LANES), BF16)],
        [VMEM] * 3,
        name="sum_plane",
    )(pack, kept, swap(n_feat, sent, 2))
    x_last = swap(n_feat, x_peer, 1)
    exact, message = call(
        sum_line_kernel,
        [(block, F32), ((2 * line * width + INTS, LANES), BF16)],
        [ANY] + [VMEM] * line,
        name="sum_line",
    )(x_peer, message, *[swap(n_feat, message, 4 * z) for z in range(1, line)])
    plane = [swap(n_feat, message, r) for r in (n_feat + 2, 2, n_feat)]
    plane = [message, *plane[::-1]]

    half = (devices // 2) * OWN
    own_counts, swapped, kept = call(
        functools.partial(last_kernel, n_feat),
        [((OWN, width), F32), ((2 * HID + width, HID), BF16), ((width, HID), F32)],
        [VMEM] * 9,
        [
            pltpu.VMEM((half, HID), BF16),
            pltpu.VMEM((half, HID), BF16),
            pltpu.VMEM((half, HID), F32),
            pltpu.VMEM((4, INTS, LANES), BF16),
            pltpu.VMEM((4, width, LANES), F32),
            pltpu.VMEM((LANES, width), F32),
            pltpu.VMEM((half, HID), BF16),
            pltpu.VMEM((2 * half, HID), BF16),
            pltpu.VMEM((2, 2 * width, rows), BF16),
        ],
        name="last",
    )(*plane, w_second, x_mine, x_core, x_peer, x_last)
    (layer_out,) = call(
        functools.partial(out_kernel, n_feat),
        [((OWN, HID), BF16)],
        [VMEM] * 4,
        [pltpu.VMEM((width, HID), BF16)],
        name="out",
    )(plane[1], exact, own_counts, w_second)
    grad_second, grad_first = call(
        add_kernel,
        [((2, HID, HID), F32), ((width, HID), F32)],
        [VMEM] * 3,
        name="add",
    )(swapped, swap(n_feat, swapped, 1), kept)
    return (layer_out, grad_second, grad_first.reshape(2, OWN, HID))


def body(features, w_first, w_second, cotangent, nbr_first, send_rows, nbr_second):
    high = lax.Precision.HIGHEST
    targets = nbr_first.shape[0]
    gathered = features[nbr_first].astype(F32)
    mean_all = (jnp.sum(gathered, axis=1) / FAN1).astype(BF16)
    self_all = features[:targets]
    term = jnp.dot(self_all, w_first[0], preferred_element_type=F32)
    pre_one = lax.psum_scatter(
        term + jnp.dot(mean_all, w_first[1], preferred_element_type=F32),
        "feat",
        scatter_dimension=0,
        tiled=True,
    )
    hidden = jax.nn.silu(pre_one).astype(BF16)
    slot_rows = send_rows[0]
    valid = (slot_rows >= 0)[..., None]
    picked = hidden[jnp.maximum(slot_rows, 0)]
    outgoing_rows = jnp.where(valid, picked, jnp.zeros_like(picked))
    received = lax.all_to_all(outgoing_rows, "graph", split_axis=0, concat_axis=0, tiled=True)
    ext = jnp.concatenate([hidden, received.reshape(-1, HID)], axis=0)
    width = ext.shape[0]
    counts = jnp.zeros((OWN, width), F32)
    for k in range(FAN2):
        counts = counts + (nbr_second[:, k, None] == jnp.arange(width)[None, :]).astype(F32)
    mean_two = (jnp.dot(counts.astype(BF16), ext, preferred_element_type=F32) / FAN2).astype(BF16)
    layer_out = jnp.dot(hidden, w_second[0], preferred_element_type=F32)
    layer_out = (layer_out + jnp.dot(mean_two, w_second[1], preferred_element_type=F32)).astype(BF16)
    grad_terms = jnp.stack(
        [
            jnp.einsum("rh,ro->ho", hidden, cotangent, preferred_element_type=F32),
            jnp.einsum("rh,ro->ho", mean_two, cotangent, preferred_element_type=F32),
        ]
    )
    grad_second = lax.psum(grad_terms, AXES)
    d_self = jnp.einsum("ro,ho->rh", cotangent, w_second[0], preferred_element_type=F32)
    d_mean = jnp.einsum("ro,ho->rh", cotangent, w_second[1], preferred_element_type=F32) / FAN2
    d_ext = jnp.dot(counts.T, d_mean, precision=high)
    halo_grad = d_ext[OWN:].reshape(-1, slot_rows.shape[1], HID).astype(BF16)
    returned = lax.all_to_all(halo_grad, "graph", split_axis=0, concat_axis=0, tiled=True)
    onehot = (slot_rows.reshape(-1)[:, None] == jnp.arange(OWN)[None, :]).astype(BF16)
    d_back = jnp.einsum("sr,sh->rh", onehot, returned.reshape(-1, HID), preferred_element_type=F32)
    d_hidden = d_self + d_ext[:OWN] + d_back
    d_pre = (d_hidden * silu_grad(pre_one)).astype(BF16)
    piece = lax.all_gather(d_pre, "feat", axis=0, tiled=True)
    first_sum = jnp.einsum("rf,rh->fh", self_all, piece, preferred_element_type=F32)
    second_sum = jnp.einsum("rf,rh->fh", mean_all, piece, preferred_element_type=F32)
    grad_first = lax.psum(jnp.stack([first_sum, second_sum]), "graph")
    return (layer_out, grad_second, grad_first)


def solution(mesh):
    n_graph = mesh.shape["graph"]
    n_feat = mesh.shape["feat"]
    in_specs = (
        P("graph", "feat"),
        P(None, "feat", None),
        P(),
        P(AXES, None),
        P("graph", None),
        P(AXES, None, None),
        P(AXES, None),
    )
    out_specs = (P(AXES, None), P(), P(None, "feat", None))
    two = n_graph == 2 and n_feat == 16
    chosen = functools.partial(pair_body, n_feat) if two else body
    return jax.shard_map(chosen, mesh=mesh, in_specs=in_specs, out_specs=out_specs, check_vma=False)
```

```python
import functools

import jax
import jax.numpy as jnp
from jax import lax
from jax.experimental import pallas as pl
from jax.experimental.pallas import tpu as pltpu
from jax.sharding import PartitionSpec as P

HID = 256
FAN1 = 15
FAN2 = 10
OWN = 32
HALO = 8
LANES = 128
INTS = 16
F32 = jnp.float32
BF16 = jnp.bfloat16
AXES = ("graph", "feat")
PLANE = ((0, 0), (1, 0), (0, 1), (1, 1))


def silu_grad(value):
    sig = jax.nn.sigmoid(value)
    return sig * (1.0 + value * (1.0 - sig))


def dot(a, b, contract):
    return lax.dot_general(a, b, (contract, ((), ())), preferred_element_type=F32)


def write_pack(sends, cot, near, pack):
    my_z = lax.axis_index("feat") // 4
    for side in range(2):
        pack[side * OWN : (side + 1) * OWN, :] = cot[:, side * LANES : (side + 1) * LANES]
    lane = lax.broadcasted_iota(jnp.int32, (INTS, LANES), 1)
    row = lax.broadcasted_iota(jnp.int32, (INTS, LANES), 0)
    lists = jnp.concatenate([near[...], jnp.zeros((INTS - FAN2, OWN), jnp.int32)], axis=0)
    ints = jnp.where(lane // OWN == my_z, jnp.concatenate([lists] * (LANES // OWN), axis=1), 0)
    for g in range(2):
        for s in range(HALO):
            here = (row == FAN2) & (lane == my_z * OWN + g * HALO + s)
            ints = jnp.where(here, sends[0, g, s], ints)
    pack[2 * OWN : 2 * OWN + INTS, :] = ints.astype(F32).astype(BF16)


def count_kernel(
    feat_hbm, nbr_hbm, w_hbm, cot_hbm, near_hbm, sends_hbm, counts, feat_t, w_first, pack, nbr_t, cot, near, sends, sems,
):
    pairs = ((nbr_hbm, nbr_t), (feat_hbm, feat_t), (w_hbm, w_first), (cot_hbm, cot), (near_hbm, near), (sends_hbm, sends))
    copies = [pltpu.make_async_copy(src, dst, sems.at[i]) for i, (src, dst) in enumerate(pairs)]
    for copy in copies:
        copy.start()
    copies[0].wait()
    row = lax.broadcasted_iota(jnp.int32, (LANES, LANES), 0)
    for t in range(nbr_t.shape[1] // LANES):
        cols = slice(t * LANES, (t + 1) * LANES)
        low = nbr_t[:, cols] & (LANES - 1)
        unit = jnp.left_shift(1, 4 * jnp.right_shift(nbr_t[:, cols], 7))
        packed = jnp.zeros((LANES, LANES), jnp.int32)
        for k in range(FAN1):
            packed = packed + jnp.where(row == low[k : k + 1, :], unit[k : k + 1, :], 0)
        for b in range(counts.shape[0] // LANES):
            part = jnp.right_shift(packed, 4 * b) & 15
            counts[b * LANES : (b + 1) * LANES, cols] = part.astype(F32).astype(BF16)
    for copy in copies[1:]:
        copy.wait()
    write_pack(sends, cot, near, pack)


def first_kernel(counts, feat_mine, w_mine, feat_core, w_core, x_t, kept, sent, share):
    line = x_t.shape[0]
    mean = [(dot(feat[...], counts[...], ((1,), (0,))) / FAN1).astype(BF16) for feat in (feat_mine, feat_core)]
    w_first = jnp.concatenate([w_mine[...], w_core[...]], axis=0)
    for t in range(line):
        cols = slice(t * LANES, (t + 1) * LANES)
        chunk = jnp.concatenate([feat_mine[:, cols], mean[0][:, cols], feat_core[:, cols], mean[1][:, cols]], axis=0)
        x_t[t] = chunk
        share[cols, :] = dot(chunk, w_first, ((0,), (0,)))
    my_feat = lax.axis_index("feat")
    for y, out in enumerate((kept, sent)):
        for z in range(line):
            owner = z * 4 + ((my_feat % 4) ^ (2 * y))
            block = share[pl.ds(pl.multiple_of(owner * OWN, OWN), OWN), :].astype(out.dtype)
            for side in range(2):
                out[z, side * OWN : (side + 1) * OWN, :] = block[:, side * LANES : (side + 1) * LANES]


def sum_plane_kernel(pack, mine, received, message):
    total = (mine[...] + received[...].astype(F32)).astype(BF16)
    rows = total.shape[0] * total.shape[1]
    message[0:rows, :] = total.reshape(rows, LANES)
    message[rows:, :] = pack[...]


def sum_line_kernel(after, *refs):
    parts, (exact, message) = refs[:-2], refs[-2:]
    my_z = lax.axis_index("feat") // 4
    line, width = exact.shape[0], exact.shape[1]
    rows = line * width
    sums = [part[0:rows, :].astype(F32) for part in parts]
    while len(sums) > 1:
        sums = [a + b for a, b in zip(sums[::2], sums[1::2])]
    total = sums[0].reshape(exact.shape)
    exact[...] = total
    total = total.astype(BF16)
    for z, part in enumerate(parts):
        message[2 * z * width : (2 * z + 1) * width, :] = total[z]
        at = pl.multiple_of((2 * (my_z ^ z) + 1) * width, width)
        message[pl.ds(at, width), :] = part[rows : rows + width, :]
    lists = [part[rows + width :, :].astype(F32) for part in parts]
    message[2 * rows :, :] = functools.reduce(lambda a, b: a + b, lists).astype(BF16)


def write_back(n_feat, plane_0, plane_1, plane_2, plane_3, w_second, cot_all, near_cot, d_hidden, own_counts, lists, spread, turn):
    line = n_feat // 4
    width = 2 * OWN
    my_graph = lax.axis_index("graph")
    my_z = lax.axis_index("feat") // 4
    my_y = lax.axis_index("feat") // 2 % 2
    for (x, y), message in zip(PLANE, (plane_0, plane_1, plane_2, plane_3)):
        at = (my_graph ^ x) * 2 + (my_y ^ y)
        lists[at] = message[2 * line * width :, :]
        for z in range(line):
            span = pl.ds(pl.multiple_of(at * LANES + z * OWN, OWN), OWN)
            for side in range(2):
                top = (2 * z + 1) * width + side * OWN
                cot_all[span, side * LANES : (side + 1) * LANES] = message[top : top + OWN, :]

    ints = lists[...].reshape(4 * INTS, LANES)
    source = lax.broadcasted_iota(jnp.int32, (LANES, LANES), 0)
    start = lax.broadcasted_iota(jnp.int32, (LANES, LANES), 1) // OWN * OWN
    pick = jnp.concatenate([jnp.where(source == start + s, 1.0, 0.0).astype(BF16) for s in range(2 * HALO)], axis=1)
    sent = dot(ints, pick, ((1,), (0,)))

    z_of = lax.broadcasted_iota(jnp.int32, (width, LANES), 1) // OWN
    slot_ix = lax.broadcasted_iota(jnp.int32, (width, LANES), 0).astype(F32)
    for y in range(2):
        total = jnp.zeros((line * width, HID), F32)
        for g in range(2):
            at = g * 2 + y
            entries = ints[at * INTS : (at + 1) * INTS, :].astype(F32)
            place_of = entries + float(g * OWN)
            for p in range(2):
                for s in range(HALO):
                    row = (p * 2 + y) * INTS + FAN2
                    there = sent[row : row + 1, (g * HALO + s) * LANES : (g * HALO + s + 1) * LANES] + p * OWN
                    place_of = jnp.where(entries == float(OWN + p * HALO + s), there, place_of)
            counts = jnp.zeros((width, LANES), F32)
            for k in range(FAN2):
                counts = counts + jnp.where(slot_ix == place_of[k : k + 1, :], 1.0, 0.0)
            spread[at] = counts
            block = jnp.concatenate([jnp.where(z_of == z, counts, 0.0) for z in range(line)], axis=0).astype(BF16)
            total = total + dot(block, cot_all[at * LANES : (at + 1) * LANES, :], ((1,), (0,)))
        total = (total / FAN2).astype(BF16)
        for z in range(line):
            for p in range(2):
                at = (p * 2 + y) * LANES + z * OWN
                near_cot[at : at + OWN, :] = total[z * width + p * OWN : z * width + (p + 1) * OWN, :]

    turn[...] = spread[pl.ds(my_graph * 2 + my_y, 1)][0].T
    own_counts[...] = turn[pl.ds(pl.multiple_of(my_z * OWN, OWN), OWN), :]

    part = dot(cot_all[...], w_second[0], ((1,), (1,)))
    d_hidden[...] = part + dot(near_cot[...], w_second[1], ((1,), (1,)))


def out_kernel(n_feat, peer, exact, own_counts, w_second, layer_out, ext):
    my_graph = lax.axis_index("graph")
    my_z = lax.axis_index("feat") // 4
    own = exact[pl.ds(my_z, 1)][0]
    far = peer[pl.ds(pl.multiple_of(my_z * 4 * OWN, 4 * OWN), 2 * OWN), :].astype(F32)
    hiddens = []
    for value in (own, far):
        value = jnp.concatenate([value[0:OWN, :], value[OWN : 2 * OWN, :]], axis=1)
        hiddens.append((value * (0.5 + 0.5 * jnp.tanh(0.5 * value))).astype(BF16))
    ext[pl.ds(pl.multiple_of(my_graph * OWN, OWN), OWN), :] = hiddens[0]
    ext[pl.ds(pl.multiple_of((1 - my_graph) * OWN, OWN), OWN), :] = hiddens[1]
    mean = (dot(own_counts[...].astype(BF16), ext[...], ((1,), (0,))) / FAN2).astype(BF16)
    out = dot(hiddens[0], w_second[0], ((1,), (0,))) + dot(mean, w_second[1], ((1,), (0,)))
    layer_out[...] = out.astype(BF16)


def last_kernel(
    n_feat, plane_0, plane_1, plane_2, plane_3, w_second, x_mine, x_peer,
    own_counts, swapped, kept, cot, near_cot, d_hidden, lists, spread, turn, hidden, d_pre, slices,
):
    write_back(n_feat, plane_0, plane_1, plane_2, plane_3, w_second, cot, near_cot, d_hidden, own_counts, lists, spread, turn)
    my_graph = lax.axis_index("graph")
    my_feat = lax.axis_index("feat")
    rows = n_feat * OWN
    half = rows // 2
    line = n_feat // 4
    d_pre[...] = jnp.zeros_like(d_pre)
    my_y = my_feat // 2 % 2
    for (x, y), message in zip(PLANE, (plane_0, plane_1, plane_2, plane_3)):
        graph = my_graph ^ x
        for z in range(line):
            span = pl.ds(pl.multiple_of((graph * 2 + (my_y ^ y)) * LANES + z * OWN, OWN), OWN)
            top = 4 * z * OWN
            value = jnp.concatenate([message[top : top + OWN, :], message[top + OWN : top + 2 * OWN, :]], axis=1).astype(F32)
            sig = 0.5 + 0.5 * jnp.tanh(0.5 * value)
            hidden[span, :] = (value * sig).astype(BF16)
            slope = sig * (1.0 + value * (1.0 - sig))
            target = pl.ds(pl.multiple_of(graph * rows + (z * 4 + (my_feat % 4 ^ 2 * y)) * OWN, OWN), OWN)
            d_pre[target, :] = (d_hidden[span, :] * slope).astype(BF16)

    swapped[0:HID, :] = dot(hidden[...], cot[...], ((0,), (0,))).astype(BF16)
    swapped[HID : 2 * HID, :] = dot(hidden[...], near_cot[...], ((0,), (0,))).astype(BF16)

    for z in range(line):
        cols = slice(z * LANES, (z + 1) * LANES)
        slices[0, :, cols] = x_mine[z]
        slices[1, :, cols] = x_peer[z]
    mine = d_pre[pl.ds(pl.multiple_of(my_graph * rows, rows), rows), :]
    peer = d_pre[pl.ds(pl.multiple_of((1 - my_graph) * rows, rows), rows), :]
    first = dot(slices[0], mine, ((1,), (0,))) + dot(slices[1], peer, ((1,), (0,)))
    kept[...] = first[0 : 2 * OWN, :]
    swapped[2 * HID : 2 * HID + 2 * OWN, :] = first[2 * OWN : 4 * OWN, :].astype(BF16)


def add_kernel(mine, theirs, kept, grad_second, grad_first):
    for w in range(2):
        span = slice(w * HID, (w + 1) * HID)
        grad_second[w] = mine[span, :].astype(F32) + theirs[span, :].astype(F32)
    grad_first[...] = kept[...] + theirs[2 * HID : 2 * HID + 2 * OWN, :].astype(F32)


VMEM = pl.BlockSpec(memory_space=pltpu.VMEM)
ANY = pl.BlockSpec(memory_space=pl.ANY)
SMEM = pl.BlockSpec(memory_space=pltpu.SMEM)
LIMIT = 40 * 1024 * 1024


def call(kernel, outs, ins, scratch=(), name=None, aliases=None):
    return pl.pallas_call(
        kernel,
        out_shape=[jax.ShapeDtypeStruct(shape, dtype) for shape, dtype in outs],
        in_specs=ins,
        out_specs=[VMEM] * len(outs),
        scratch_shapes=list(scratch),
        input_output_aliases=aliases or {},
        compiler_params=pltpu.CompilerParams(vmem_limit_bytes=LIMIT),
        name=name,
    )


def swap(n_feat, value, relative):
    return lax.ppermute(value, AXES, [(d, d ^ relative) for d in range(2 * n_feat)])


def pair_body(n_feat, features, w_first, w_second, cotangent, nbr_first, send_rows, nbr_second):
    devices = 2 * n_feat
    rows = n_feat * OWN
    width = 2 * OWN
    line = n_feat // 4
    from_hbm = [features.T, nbr_first.T, w_first.reshape(width, HID), cotangent, nbr_second.T, send_rows]
    block = (line, width, LANES)
    sources = features.shape[0]
    counts, feat_mine, w_mine, pack = call(
        count_kernel,
        [((sources, rows), BF16), ((OWN, sources), BF16), ((width, HID), BF16), ((width + INTS, LANES), BF16)],
        [ANY] * 6,
        [pltpu.VMEM(x.shape, x.dtype) for x in (nbr_first.T, cotangent, nbr_second.T)]
        + [pltpu.SMEM(send_rows.shape, jnp.int32), pltpu.SemaphoreType.DMA((6,))],
        name="count",
    )(*[pltpu.with_memory_space_constraint(x, pltpu.HBM) for x in from_hbm])
    x_mine, kept, sent = call(
        first_kernel,
        [((line, 2 * width, LANES), BF16), (block, F32), (block, BF16)],
        [VMEM] * 5,
        [pltpu.VMEM((rows, HID), F32)],
        name="first",
    )(counts, feat_mine, w_mine, swap(n_feat, from_hbm[0], 1), swap(n_feat, from_hbm[2], 1))
    x_peer = swap(n_feat, x_mine, n_feat)
    (message,) = call(
        sum_plane_kernel,
        [((line * width + width + INTS, LANES), BF16)],
        [VMEM] * 3,
        name="sum_plane",
    )(pack, kept, swap(n_feat, sent, 2))
    exact, message = call(
        sum_line_kernel,
        [(block, F32), ((2 * line * width + INTS, LANES), BF16)],
        [ANY] + [VMEM] * line,
        name="sum_line",
    )(x_peer, message, *[swap(n_feat, message, 4 * z) for z in range(1, line)])
    plane = [swap(n_feat, message, r) for r in (n_feat + 2, 2, n_feat)]
    plane = [message, *plane[::-1]]

    half = (devices // 2) * OWN
    own_counts, swapped, kept = call(
        functools.partial(last_kernel, n_feat),
        [((OWN, width), F32), ((2 * HID + width, HID), BF16), ((width, HID), F32)],
        [VMEM] * 7,
        [
            pltpu.VMEM((half, HID), BF16),
            pltpu.VMEM((half, HID), BF16),
            pltpu.VMEM((half, HID), F32),
            pltpu.VMEM((4, INTS, LANES), BF16),
            pltpu.VMEM((4, width, LANES), F32),
            pltpu.VMEM((LANES, width), F32),
            pltpu.VMEM((half, HID), BF16),
            pltpu.VMEM((2 * half, HID), BF16),
            pltpu.VMEM((2, 2 * width, rows), BF16),
        ],
        name="last",
    )(*plane, w_second, x_mine, x_peer)
    (layer_out,) = call(
        functools.partial(out_kernel, n_feat),
        [((OWN, HID), BF16)],
        [VMEM] * 4,
        [pltpu.VMEM((width, HID), BF16)],
        name="out",
    )(plane[1], exact, own_counts, w_second)
    grad_second, grad_first = call(
        add_kernel,
        [((2, HID, HID), F32), ((width, HID), F32)],
        [VMEM] * 3,
        name="add",
    )(swapped, swap(n_feat, swapped, 1), kept)
    return (layer_out, grad_second, grad_first.reshape(2, OWN, HID))


def body(features, w_first, w_second, cotangent, nbr_first, send_rows, nbr_second):
    high = lax.Precision.HIGHEST
    targets = nbr_first.shape[0]
    gathered = features[nbr_first].astype(F32)
    mean_all = (jnp.sum(gathered, axis=1) / FAN1).astype(BF16)
    self_all = features[:targets]
    term = jnp.dot(self_all, w_first[0], preferred_element_type=F32)
    pre_one = lax.psum_scatter(
        term + jnp.dot(mean_all, w_first[1], preferred_element_type=F32),
        "feat",
        scatter_dimension=0,
        tiled=True,
    )
    hidden = jax.nn.silu(pre_one).astype(BF16)
    slot_rows = send_rows[0]
    valid = (slot_rows >= 0)[..., None]
    picked = hidden[jnp.maximum(slot_rows, 0)]
    outgoing_rows = jnp.where(valid, picked, jnp.zeros_like(picked))
    received = lax.all_to_all(outgoing_rows, "graph", split_axis=0, concat_axis=0, tiled=True)
    ext = jnp.concatenate([hidden, received.reshape(-1, HID)], axis=0)
    width = ext.shape[0]
    counts = jnp.zeros((OWN, width), F32)
    for k in range(FAN2):
        counts = counts + (nbr_second[:, k, None] == jnp.arange(width)[None, :]).astype(F32)
    mean_two = (jnp.dot(counts.astype(BF16), ext, preferred_element_type=F32) / FAN2).astype(BF16)
    layer_out = jnp.dot(hidden, w_second[0], preferred_element_type=F32)
    layer_out = (layer_out + jnp.dot(mean_two, w_second[1], preferred_element_type=F32)).astype(BF16)
    grad_terms = jnp.stack(
        [
            jnp.einsum("rh,ro->ho", hidden, cotangent, preferred_element_type=F32),
            jnp.einsum("rh,ro->ho", mean_two, cotangent, preferred_element_type=F32),
        ]
    )
    grad_second = lax.psum(grad_terms, AXES)
    d_self = jnp.einsum("ro,ho->rh", cotangent, w_second[0], preferred_element_type=F32)
    d_mean = jnp.einsum("ro,ho->rh", cotangent, w_second[1], preferred_element_type=F32) / FAN2
    d_ext = jnp.dot(counts.T, d_mean, precision=high)
    halo_grad = d_ext[OWN:].reshape(-1, slot_rows.shape[1], HID).astype(BF16)
    returned = lax.all_to_all(halo_grad, "graph", split_axis=0, concat_axis=0, tiled=True)
    onehot = (slot_rows.reshape(-1)[:, None] == jnp.arange(OWN)[None, :]).astype(BF16)
    d_back = jnp.einsum("sr,sh->rh", onehot, returned.reshape(-1, HID), preferred_element_type=F32)
    d_hidden = d_self + d_ext[:OWN] + d_back
    d_pre = (d_hidden * silu_grad(pre_one)).astype(BF16)
    piece = lax.all_gather(d_pre, "feat", axis=0, tiled=True)
    first_sum = jnp.einsum("rf,rh->fh", self_all, piece, preferred_element_type=F32)
    second_sum = jnp.einsum("rf,rh->fh", mean_all, piece, preferred_element_type=F32)
    grad_first = lax.psum(jnp.stack([first_sum, second_sum]), "graph")
    return (layer_out, grad_second, grad_first)


def solution(mesh):
    n_graph = mesh.shape["graph"]
    n_feat = mesh.shape["feat"]
    in_specs = (
        P("graph", "feat"),
        P(None, "feat", None),
        P(),
        P(AXES, None),
        P("graph", None),
        P(AXES, None, None),
        P(AXES, None),
    )
    out_specs = (P(AXES, None), P(), P(None, "feat", None))
    two = n_graph == 2 and n_feat == 16
    chosen = functools.partial(pair_body, n_feat) if two else body
    return jax.shard_map(chosen, mesh=mesh, in_specs=in_specs, out_specs=out_specs, check_vma=False)
```

```python
import functools

import jax
import jax.numpy as jnp
from jax import lax
from jax.experimental import pallas as pl
from jax.experimental.pallas import tpu as pltpu
from jax.sharding import PartitionSpec as P

HID = 256
FAN1 = 15
FAN2 = 10
OWN = 32
HALO = 8
LANES = 128
INTS = 16
F32 = jnp.float32
BF16 = jnp.bfloat16
AXES = ("graph", "feat")
PLANE = ((0, 0), (1, 0), (0, 1), (1, 1))


def silu_grad(value):
    sig = jax.nn.sigmoid(value)
    return sig * (1.0 + value * (1.0 - sig))


def dot(a, b, contract):
    return lax.dot_general(a, b, (contract, ((), ())), preferred_element_type=F32)


def write_pack(sends, cot, near, pack):
    my_z = lax.axis_index("feat") // 4
    for side in range(2):
        pack[side * OWN : (side + 1) * OWN, :] = cot[:, side * LANES : (side + 1) * LANES]
    lane = lax.broadcasted_iota(jnp.int32, (INTS, LANES), 1)
    row = lax.broadcasted_iota(jnp.int32, (INTS, LANES), 0)
    lists = jnp.concatenate([near[...], jnp.zeros((INTS - FAN2, OWN), jnp.int32)], axis=0)
    ints = jnp.where(lane // OWN == my_z, jnp.concatenate([lists] * (LANES // OWN), axis=1), 0)
    for g in range(2):
        for s in range(HALO):
            here = (row == FAN2) & (lane == my_z * OWN + g * HALO + s)
            ints = jnp.where(here, sends[0, g, s], ints)
    pack[2 * OWN : 2 * OWN + INTS, :] = ints.astype(F32).astype(BF16)


def count_kernel(
    feat_hbm, nbr_hbm, w_hbm, cot_hbm, near_hbm, sends_hbm, counts, feat_t, w_first, pack, nbr_t, cot, near, sends, sems,
):
    pairs = ((nbr_hbm, nbr_t), (feat_hbm, feat_t), (w_hbm, w_first), (cot_hbm, cot), (near_hbm, near), (sends_hbm, sends))
    copies = [pltpu.make_async_copy(src, dst, sems.at[i]) for i, (src, dst) in enumerate(pairs)]
    for copy in copies:
        copy.start()
    copies[0].wait()
    row = lax.broadcasted_iota(jnp.int32, (LANES, LANES), 0)
    for t in range(nbr_t.shape[1] // LANES):
        cols = slice(t * LANES, (t + 1) * LANES)
        low = nbr_t[:, cols] & (LANES - 1)
        unit = jnp.left_shift(1, 4 * jnp.right_shift(nbr_t[:, cols], 7))
        packed = jnp.zeros((LANES, LANES), jnp.int32)
        for k in range(FAN1):
            packed = packed + jnp.where(row == low[k : k + 1, :], unit[k : k + 1, :], 0)
        for b in range(counts.shape[0] // LANES):
            part = jnp.right_shift(packed, 4 * b) & 15
            counts[b * LANES : (b + 1) * LANES, cols] = part.astype(F32).astype(BF16)
    for copy in copies[1:]:
        copy.wait()
    write_pack(sends, cot, near, pack)


def first_kernel(counts, feat_mine, w_mine, feat_core, w_core, x_t, kept, sent, share):
    line = x_t.shape[0]
    both = jnp.concatenate([feat_mine[...], feat_core[...]], axis=0)
    mean = (dot(both, counts[...], ((1,), (0,))) / FAN1).astype(BF16)
    w_first = jnp.concatenate([w_mine[...], w_core[...]], axis=0)
    for t in range(line):
        cols = slice(t * LANES, (t + 1) * LANES)
        chunk = jnp.concatenate([both[0:OWN, cols], mean[0:OWN, cols], both[OWN:, cols], mean[OWN:, cols]], axis=0)
        x_t[t] = chunk
        share[cols, :] = dot(chunk, w_first, ((0,), (0,)))
    my_feat = lax.axis_index("feat")
    for y, out in enumerate((kept, sent)):
        for z in range(line):
            owner = z * 4 + ((my_feat % 4) ^ (2 * y))
            block = share[pl.ds(pl.multiple_of(owner * OWN, OWN), OWN), :].astype(out.dtype)
            for side in range(2):
                out[z, side * OWN : (side + 1) * OWN, :] = block[:, side * LANES : (side + 1) * LANES]


def sum_plane_kernel(pack, mine, received, message):
    total = (mine[...] + received[...].astype(F32)).astype(BF16)
    rows = total.shape[0] * total.shape[1]
    message[0:rows, :] = total.reshape(rows, LANES)
    message[rows:, :] = pack[...]


def sum_line_kernel(after, *refs):
    parts, (exact, message) = refs[:-2], refs[-2:]
    my_z = lax.axis_index("feat") // 4
    line, width = exact.shape[0], exact.shape[1]
    rows = line * width
    sums = [part[0:rows, :].astype(F32) for part in parts]
    while len(sums) > 1:
        sums = [a + b for a, b in zip(sums[::2], sums[1::2])]
    total = sums[0].reshape(exact.shape)
    exact[...] = total
    total = total.astype(BF16)
    for z, part in enumerate(parts):
        message[2 * z * width : (2 * z + 1) * width, :] = total[z]
        at = pl.multiple_of((2 * (my_z ^ z) + 1) * width, width)
        message[pl.ds(at, width), :] = part[rows : rows + width, :]
    lists = [part[rows + width :, :].astype(F32) for part in parts]
    message[2 * rows :, :] = functools.reduce(lambda a, b: a + b, lists).astype(BF16)


def write_back(n_feat, plane_0, plane_1, plane_2, plane_3, w_second, cots, d_hidden, own_counts, lists, spread, turn):
    line = n_feat // 4
    width = 2 * OWN
    my_graph = lax.axis_index("graph")
    my_z = lax.axis_index("feat") // 4
    my_y = lax.axis_index("feat") // 2 % 2
    for (x, y), message in zip(PLANE, (plane_0, plane_1, plane_2, plane_3)):
        at = (my_graph ^ x) * 2 + (my_y ^ y)
        lists[at] = message[2 * line * width :, :]
        for z in range(line):
            span = pl.ds(pl.multiple_of(at * LANES + z * OWN, OWN), OWN)
            for side in range(2):
                top = (2 * z + 1) * width + side * OWN
                cots[span, side * LANES : (side + 1) * LANES] = message[top : top + OWN, :]

    ints = lists[...].reshape(4 * INTS, LANES)
    source = lax.broadcasted_iota(jnp.int32, (LANES, LANES), 0)
    start = lax.broadcasted_iota(jnp.int32, (LANES, LANES), 1) // OWN * OWN
    pick = jnp.concatenate([jnp.where(source == start + s, 1.0, 0.0).astype(BF16) for s in range(2 * HALO)], axis=1)
    sent = dot(ints, pick, ((1,), (0,)))

    z_of = lax.broadcasted_iota(jnp.int32, (width, LANES), 1) // OWN
    slot_ix = lax.broadcasted_iota(jnp.int32, (width, LANES), 0).astype(F32)
    for y in range(2):
        total = jnp.zeros((line * width, HID), F32)
        for g in range(2):
            at = g * 2 + y
            entries = ints[at * INTS : (at + 1) * INTS, :].astype(F32)
            place_of = entries + float(g * OWN)
            for p in range(2):
                for s in range(HALO):
                    row = (p * 2 + y) * INTS + FAN2
                    there = sent[row : row + 1, (g * HALO + s) * LANES : (g * HALO + s + 1) * LANES] + p * OWN
                    place_of = jnp.where(entries == float(OWN + p * HALO + s), there, place_of)
            counts = jnp.zeros((width, LANES), F32)
            for k in range(FAN2):
                counts = counts + jnp.where(slot_ix == place_of[k : k + 1, :], 1.0, 0.0)
            spread[at] = counts
            block = jnp.concatenate([jnp.where(z_of == z, counts, 0.0) for z in range(line)], axis=0).astype(BF16)
            total = total + dot(block, cots[at * LANES : (at + 1) * LANES, 0:HID], ((1,), (0,)))
        total = (total / FAN2).astype(BF16)
        for z in range(line):
            for p in range(2):
                at = (p * 2 + y) * LANES + z * OWN
                cots[at : at + OWN, HID : 2 * HID] = total[z * width + p * OWN : z * width + (p + 1) * OWN, :]

    turn[...] = spread[pl.ds(my_graph * 2 + my_y, 1)][0].T
    own_counts[...] = turn[pl.ds(pl.multiple_of(my_z * OWN, OWN), OWN), :]

    weights = jnp.concatenate([w_second[0], w_second[1]], axis=1)
    d_hidden[...] = dot(cots[...], weights, ((1,), (1,)))


def out_kernel(n_feat, peer, exact, own_counts, w_second, layer_out, ext):
    my_graph = lax.axis_index("graph")
    my_z = lax.axis_index("feat") // 4
    own = exact[pl.ds(my_z, 1)][0]
    far = peer[pl.ds(pl.multiple_of(my_z * 4 * OWN, 4 * OWN), 2 * OWN), :].astype(F32)
    hiddens = []
    for value in (own, far):
        value = jnp.concatenate([value[0:OWN, :], value[OWN : 2 * OWN, :]], axis=1)
        hiddens.append((value * (0.5 + 0.5 * jnp.tanh(0.5 * value))).astype(BF16))
    ext[pl.ds(pl.multiple_of(my_graph * OWN, OWN), OWN), :] = hiddens[0]
    ext[pl.ds(pl.multiple_of((1 - my_graph) * OWN, OWN), OWN), :] = hiddens[1]
    mean = (dot(own_counts[...].astype(BF16), ext[...], ((1,), (0,))) / FAN2).astype(BF16)
    out = dot(hiddens[0], w_second[0], ((1,), (0,))) + dot(mean, w_second[1], ((1,), (0,)))
    layer_out[...] = out.astype(BF16)


def last_kernel(
    n_feat, plane_0, plane_1, plane_2, plane_3, w_second, x_mine, x_peer,
    own_counts, swapped, kept, cots, d_hidden, lists, spread, turn, hidden, d_pre, slices,
):
    write_back(n_feat, plane_0, plane_1, plane_2, plane_3, w_second, cots, d_hidden, own_counts, lists, spread, turn)
    my_graph = lax.axis_index("graph")
    my_feat = lax.axis_index("feat")
    rows = n_feat * OWN
    half = rows // 2
    line = n_feat // 4
    d_pre[...] = jnp.zeros_like(d_pre)
    my_y = my_feat // 2 % 2
    for (x, y), message in zip(PLANE, (plane_0, plane_1, plane_2, plane_3)):
        graph = my_graph ^ x
        for z in range(line):
            span = pl.ds(pl.multiple_of((graph * 2 + (my_y ^ y)) * LANES + z * OWN, OWN), OWN)
            top = 4 * z * OWN
            value = jnp.concatenate([message[top : top + OWN, :], message[top + OWN : top + 2 * OWN, :]], axis=1).astype(F32)
            sig = 0.5 + 0.5 * jnp.tanh(0.5 * value)
            hidden[span, :] = (value * sig).astype(BF16)
            slope = sig * (1.0 + value * (1.0 - sig))
            target = pl.ds(pl.multiple_of(graph * rows + (z * 4 + (my_feat % 4 ^ 2 * y)) * OWN, OWN), OWN)
            d_pre[target, :] = (d_hidden[span, :] * slope).astype(BF16)

    second = dot(hidden[...], cots[...], ((0,), (0,))).astype(BF16)
    swapped[0:HID, :] = second[:, 0:HID]
    swapped[HID : 2 * HID, :] = second[:, HID : 2 * HID]

    for z in range(line):
        cols = slice(z * LANES, (z + 1) * LANES)
        slices[0, :, cols] = x_mine[z]
        slices[1, :, cols] = x_peer[z]
    mine = d_pre[pl.ds(pl.multiple_of(my_graph * rows, rows), rows), :]
    peer = d_pre[pl.ds(pl.multiple_of((1 - my_graph) * rows, rows), rows), :]
    first = dot(slices[0], mine, ((1,), (0,))) + dot(slices[1], peer, ((1,), (0,)))
    kept[...] = first[0 : 2 * OWN, :]
    swapped[2 * HID : 2 * HID + 2 * OWN, :] = first[2 * OWN : 4 * OWN, :].astype(BF16)


def add_kernel(mine, theirs, kept, grad_second, grad_first):
    for w in range(2):
        span = slice(w * HID, (w + 1) * HID)
        grad_second[w] = mine[span, :].astype(F32) + theirs[span, :].astype(F32)
    grad_first[...] = kept[...] + theirs[2 * HID : 2 * HID + 2 * OWN, :].astype(F32)


VMEM = pl.BlockSpec(memory_space=pltpu.VMEM)
ANY = pl.BlockSpec(memory_space=pl.ANY)
SMEM = pl.BlockSpec(memory_space=pltpu.SMEM)
LIMIT = 40 * 1024 * 1024


def call(kernel, outs, ins, scratch=(), name=None, aliases=None):
    return pl.pallas_call(
        kernel,
        out_shape=[jax.ShapeDtypeStruct(shape, dtype) for shape, dtype in outs],
        in_specs=ins,
        out_specs=[VMEM] * len(outs),
        scratch_shapes=list(scratch),
        input_output_aliases=aliases or {},
        compiler_params=pltpu.CompilerParams(vmem_limit_bytes=LIMIT),
        name=name,
    )


def swap(n_feat, value, relative):
    return lax.ppermute(value, AXES, [(d, d ^ relative) for d in range(2 * n_feat)])


def pair_body(n_feat, features, w_first, w_second, cotangent, nbr_first, send_rows, nbr_second):
    devices = 2 * n_feat
    rows = n_feat * OWN
    width = 2 * OWN
    line = n_feat // 4
    from_hbm = [features.T, nbr_first.T, w_first.reshape(width, HID), cotangent, nbr_second.T, send_rows]
    block = (line, width, LANES)
    sources = features.shape[0]
    counts, feat_mine, w_mine, pack = call(
        count_kernel,
        [((sources, rows), BF16), ((OWN, sources), BF16), ((width, HID), BF16), ((width + INTS, LANES), BF16)],
        [ANY] * 6,
        [pltpu.VMEM(x.shape, x.dtype) for x in (nbr_first.T, cotangent, nbr_second.T)]
        + [pltpu.SMEM(send_rows.shape, jnp.int32), pltpu.SemaphoreType.DMA((6,))],
        name="count",
    )(*[pltpu.with_memory_space_constraint(x, pltpu.HBM) for x in from_hbm])
    x_mine, kept, sent = call(
        first_kernel,
        [((line, 2 * width, LANES), BF16), (block, F32), (block, BF16)],
        [VMEM] * 5,
        [pltpu.VMEM((rows, HID), F32)],
        name="first",
    )(counts, feat_mine, w_mine, swap(n_feat, from_hbm[0], 1), swap(n_feat, from_hbm[2], 1))
    x_peer = swap(n_feat, x_mine, n_feat)
    (message,) = call(
        sum_plane_kernel,
        [((line * width + width + INTS, LANES), BF16)],
        [VMEM] * 3,
        name="sum_plane",
    )(pack, kept, swap(n_feat, sent, 2))
    exact, message = call(
        sum_line_kernel,
        [(block, F32), ((2 * line * width + INTS, LANES), BF16)],
        [ANY] + [VMEM] * line,
        name="sum_line",
    )(x_peer, message, *[swap(n_feat, message, 4 * z) for z in range(1, line)])
    plane = [swap(n_feat, message, r) for r in (n_feat + 2, 2, n_feat)]
    plane = [message, *plane[::-1]]

    half = (devices // 2) * OWN
    own_counts, swapped, kept = call(
        functools.partial(last_kernel, n_feat),
        [((OWN, width), F32), ((2 * HID + width, HID), BF16), ((width, HID), F32)],
        [VMEM] * 7,
        [
            pltpu.VMEM((half, 2 * HID), BF16),
            pltpu.VMEM((half, HID), F32),
            pltpu.VMEM((4, INTS, LANES), BF16),
            pltpu.VMEM((4, width, LANES), F32),
            pltpu.VMEM((LANES, width), F32),
            pltpu.VMEM((half, HID), BF16),
            pltpu.VMEM((2 * half, HID), BF16),
            pltpu.VMEM((2, 2 * width, rows), BF16),
        ],
        name="last",
    )(*plane, w_second, x_mine, x_peer)
    (layer_out,) = call(
        functools.partial(out_kernel, n_feat),
        [((OWN, HID), BF16)],
        [VMEM] * 4,
        [pltpu.VMEM((width, HID), BF16)],
        name="out",
    )(plane[1], exact, own_counts, w_second)
    grad_second, grad_first = call(
        add_kernel,
        [((2, HID, HID), F32), ((width, HID), F32)],
        [VMEM] * 3,
        name="add",
    )(swapped, swap(n_feat, swapped, 1), kept)
    return (layer_out, grad_second, grad_first.reshape(2, OWN, HID))


def body(features, w_first, w_second, cotangent, nbr_first, send_rows, nbr_second):
    high = lax.Precision.HIGHEST
    targets = nbr_first.shape[0]
    gathered = features[nbr_first].astype(F32)
    mean_all = (jnp.sum(gathered, axis=1) / FAN1).astype(BF16)
    self_all = features[:targets]
    term = jnp.dot(self_all, w_first[0], preferred_element_type=F32)
    pre_one = lax.psum_scatter(
        term + jnp.dot(mean_all, w_first[1], preferred_element_type=F32),
        "feat",
        scatter_dimension=0,
        tiled=True,
    )
    hidden = jax.nn.silu(pre_one).astype(BF16)
    slot_rows = send_rows[0]
    valid = (slot_rows >= 0)[..., None]
    picked = hidden[jnp.maximum(slot_rows, 0)]
    outgoing_rows = jnp.where(valid, picked, jnp.zeros_like(picked))
    received = lax.all_to_all(outgoing_rows, "graph", split_axis=0, concat_axis=0, tiled=True)
    ext = jnp.concatenate([hidden, received.reshape(-1, HID)], axis=0)
    width = ext.shape[0]
    counts = jnp.zeros((OWN, width), F32)
    for k in range(FAN2):
        counts = counts + (nbr_second[:, k, None] == jnp.arange(width)[None, :]).astype(F32)
    mean_two = (jnp.dot(counts.astype(BF16), ext, preferred_element_type=F32) / FAN2).astype(BF16)
    layer_out = jnp.dot(hidden, w_second[0], preferred_element_type=F32)
    layer_out = (layer_out + jnp.dot(mean_two, w_second[1], preferred_element_type=F32)).astype(BF16)
    grad_terms = jnp.stack(
        [
            jnp.einsum("rh,ro->ho", hidden, cotangent, preferred_element_type=F32),
            jnp.einsum("rh,ro->ho", mean_two, cotangent, preferred_element_type=F32),
        ]
    )
    grad_second = lax.psum(grad_terms, AXES)
    d_self = jnp.einsum("ro,ho->rh", cotangent, w_second[0], preferred_element_type=F32)
    d_mean = jnp.einsum("ro,ho->rh", cotangent, w_second[1], preferred_element_type=F32) / FAN2
    d_ext = jnp.dot(counts.T, d_mean, precision=high)
    halo_grad = d_ext[OWN:].reshape(-1, slot_rows.shape[1], HID).astype(BF16)
    returned = lax.all_to_all(halo_grad, "graph", split_axis=0, concat_axis=0, tiled=True)
    onehot = (slot_rows.reshape(-1)[:, None] == jnp.arange(OWN)[None, :]).astype(BF16)
    d_back = jnp.einsum("sr,sh->rh", onehot, returned.reshape(-1, HID), preferred_element_type=F32)
    d_hidden = d_self + d_ext[:OWN] + d_back
    d_pre = (d_hidden * silu_grad(pre_one)).astype(BF16)
    piece = lax.all_gather(d_pre, "feat", axis=0, tiled=True)
    first_sum = jnp.einsum("rf,rh->fh", self_all, piece, preferred_element_type=F32)
    second_sum = jnp.einsum("rf,rh->fh", mean_all, piece, preferred_element_type=F32)
    grad_first = lax.psum(jnp.stack([first_sum, second_sum]), "graph")
    return (layer_out, grad_second, grad_first)


def solution(mesh):
    n_graph = mesh.shape["graph"]
    n_feat = mesh.shape["feat"]
    in_specs = (
        P("graph", "feat"),
        P(None, "feat", None),
        P(),
        P(AXES, None),
        P("graph", None),
        P(AXES, None, None),
        P(AXES, None),
    )
    out_specs = (P(AXES, None), P(), P(None, "feat", None))
    two = n_graph == 2 and n_feat == 16
    chosen = functools.partial(pair_body, n_feat) if two else body
    return jax.shard_map(chosen, mesh=mesh, in_specs=in_specs, out_specs=out_specs, check_vma=False)
```

```python
import functools

import jax
import jax.numpy as jnp
from jax import lax
from jax.experimental import pallas as pl
from jax.experimental.pallas import tpu as pltpu
from jax.sharding import PartitionSpec as P

HID = 256
FAN1 = 15
FAN2 = 10
OWN = 32
HALO = 8
LANES = 128
INTS = 16
F32 = jnp.float32
BF16 = jnp.bfloat16
AXES = ("graph", "feat")
PLANE = ((0, 0), (1, 0), (0, 1), (1, 1))


def silu_grad(value):
    sig = jax.nn.sigmoid(value)
    return sig * (1.0 + value * (1.0 - sig))


def dot(a, b, contract):
    return lax.dot_general(a, b, (contract, ((), ())), preferred_element_type=F32)


def write_pack(sends, cot, near, pack):
    my_z = lax.axis_index("feat") // 4
    for side in range(2):
        pack[side * OWN : (side + 1) * OWN, :] = cot[:, side * LANES : (side + 1) * LANES]
    lane = lax.broadcasted_iota(jnp.int32, (INTS, LANES), 1)
    row = lax.broadcasted_iota(jnp.int32, (INTS, LANES), 0)
    lists = jnp.concatenate([near[...], jnp.zeros((INTS - FAN2, OWN), jnp.int32)], axis=0)
    ints = jnp.where(lane // OWN == my_z, jnp.concatenate([lists] * (LANES // OWN), axis=1), 0)
    for g in range(2):
        for s in range(HALO):
            here = (row == FAN2) & (lane == my_z * OWN + g * HALO + s)
            ints = jnp.where(here, sends[0, g, s], ints)
    pack[2 * OWN : 2 * OWN + INTS, :] = ints.astype(F32).astype(BF16)


def count_kernel(
    feat_hbm, nbr_hbm, w_hbm, cot_hbm, near_hbm, sends_hbm, counts, feat_t, w_first, pack, nbr_t, cot, near, sends, sems,
):
    pairs = ((nbr_hbm, nbr_t), (feat_hbm, feat_t), (w_hbm, w_first), (cot_hbm, cot), (near_hbm, near), (sends_hbm, sends))
    copies = [pltpu.make_async_copy(src, dst, sems.at[i]) for i, (src, dst) in enumerate(pairs)]
    for copy in copies:
        copy.start()
    copies[0].wait()
    row = lax.broadcasted_iota(jnp.int32, (LANES, LANES), 0)
    for t in range(nbr_t.shape[1] // LANES):
        cols = slice(t * LANES, (t + 1) * LANES)
        low = nbr_t[:, cols] & (LANES - 1)
        unit = jnp.left_shift(1, 4 * jnp.right_shift(nbr_t[:, cols], 7))
        packed = jnp.zeros((LANES, LANES), jnp.int32)
        for k in range(FAN1):
            packed = packed + jnp.where(row == low[k : k + 1, :], unit[k : k + 1, :], 0)
        for b in range(counts.shape[0] // LANES):
            part = jnp.right_shift(packed, 4 * b) & 15
            counts[b * LANES : (b + 1) * LANES, cols] = part.astype(F32).astype(BF16)
    for copy in copies[1:]:
        copy.wait()
    write_pack(sends, cot, near, pack)


def first_kernel(counts, feat_mine, w_mine, feat_core, w_core, x_t, kept, sent, share):
    line = x_t.shape[0]
    both = jnp.concatenate([feat_mine[...], feat_core[...]], axis=0)
    mean = (dot(both, counts[...], ((1,), (0,))) / FAN1).astype(BF16)
    w_first = jnp.concatenate([w_mine[...], w_core[...]], axis=0)
    for t in range(line):
        cols = slice(t * LANES, (t + 1) * LANES)
        chunk = jnp.concatenate([both[0:OWN, cols], mean[0:OWN, cols], both[OWN:, cols], mean[OWN:, cols]], axis=0)
        x_t[t] = chunk
        share[cols, :] = dot(chunk, w_first, ((0,), (0,)))
    my_feat = lax.axis_index("feat")
    for y, out in enumerate((kept, sent)):
        for z in range(line):
            owner = z * 4 + ((my_feat % 4) ^ (2 * y))
            block = share[pl.ds(pl.multiple_of(owner * OWN, OWN), OWN), :].astype(out.dtype)
            for side in range(2):
                out[z, side * OWN : (side + 1) * OWN, :] = block[:, side * LANES : (side + 1) * LANES]


def sum_plane_kernel(pack, mine, received, message):
    total = (mine[...] + received[...].astype(F32)).astype(BF16)
    rows = total.shape[0] * total.shape[1]
    message[0:rows, :] = total.reshape(rows, LANES)
    message[rows:, :] = pack[...]


def sum_line_kernel(after, *refs):
    parts, (exact, message) = (refs[0], refs[1], refs[3], refs[2]), refs[-2:]
    my_z = lax.axis_index("feat") // 4
    line, width = exact.shape[0], exact.shape[1]
    rows = line * width
    sums = [part[0:rows, :].astype(F32) for part in parts]
    while len(sums) > 1:
        sums = [a + b for a, b in zip(sums[::2], sums[1::2])]
    total = sums[0].reshape(exact.shape)
    exact[...] = total
    total = total.astype(BF16)
    for z, part in enumerate(parts):
        message[2 * z * width : (2 * z + 1) * width, :] = total[z]
        at = pl.multiple_of((2 * (my_z ^ z) + 1) * width, width)
        message[pl.ds(at, width), :] = part[rows : rows + width, :]
    lists = [part[rows + width :, :].astype(F32) for part in parts]
    message[2 * rows :, :] = functools.reduce(lambda a, b: a + b, lists).astype(BF16)


def write_back(n_feat, plane_0, plane_1, plane_2, plane_3, w_second, cots, d_hidden, own_counts, lists, spread, turn):
    line = n_feat // 4
    width = 2 * OWN
    my_graph = lax.axis_index("graph")
    my_z = lax.axis_index("feat") // 4
    my_y = lax.axis_index("feat") // 2 % 2
    for (x, y), message in zip(PLANE, (plane_0, plane_1, plane_2, plane_3)):
        at = (my_graph ^ x) * 2 + (my_y ^ y)
        lists[at] = message[2 * line * width :, :]
        for z in range(line):
            span = pl.ds(pl.multiple_of(at * LANES + z * OWN, OWN), OWN)
            for side in range(2):
                top = (2 * z + 1) * width + side * OWN
                cots[span, side * LANES : (side + 1) * LANES] = message[top : top + OWN, :]

    ints = lists[...].reshape(4 * INTS, LANES)
    source = lax.broadcasted_iota(jnp.int32, (LANES, LANES), 0)
    start = lax.broadcasted_iota(jnp.int32, (LANES, LANES), 1) // OWN * OWN
    pick = jnp.concatenate([jnp.where(source == start + s, 1.0, 0.0).astype(BF16) for s in range(2 * HALO)], axis=1)
    sent = dot(ints, pick, ((1,), (0,)))

    z_of = lax.broadcasted_iota(jnp.int32, (width, LANES), 1) // OWN
    slot_ix = lax.broadcasted_iota(jnp.int32, (width, LANES), 0).astype(F32)
    for y in range(2):
        total = jnp.zeros((line * width, HID), F32)
        for g in range(2):
            at = g * 2 + y
            entries = ints[at * INTS : (at + 1) * INTS, :].astype(F32)
            place_of = entries + float(g * OWN)
            for p in range(2):
                for s in range(HALO):
                    row = (p * 2 + y) * INTS + FAN2
                    there = sent[row : row + 1, (g * HALO + s) * LANES : (g * HALO + s + 1) * LANES] + p * OWN
                    place_of = jnp.where(entries == float(OWN + p * HALO + s), there, place_of)
            counts = jnp.zeros((width, LANES), F32)
            for k in range(FAN2):
                counts = counts + jnp.where(slot_ix == place_of[k : k + 1, :], 1.0, 0.0)
            spread[at] = counts
            block = jnp.concatenate([jnp.where(z_of == z, counts, 0.0) for z in range(line)], axis=0).astype(BF16)
            total = total + dot(block, cots[at * LANES : (at + 1) * LANES, 0:HID], ((1,), (0,)))
        total = (total / FAN2).astype(BF16)
        for z in range(line):
            for p in range(2):
                at = (p * 2 + y) * LANES + z * OWN
                cots[at : at + OWN, HID : 2 * HID] = total[z * width + p * OWN : z * width + (p + 1) * OWN, :]

    turn[...] = spread[pl.ds(my_graph * 2 + my_y, 1)][0].T
    own_counts[...] = turn[pl.ds(pl.multiple_of(my_z * OWN, OWN), OWN), :]

    weights = jnp.concatenate([w_second[0], w_second[1]], axis=1)
    d_hidden[...] = dot(cots[...], weights, ((1,), (1,)))


def out_kernel(n_feat, peer, exact, own_counts, w_second, layer_out, ext):
    my_graph = lax.axis_index("graph")
    my_z = lax.axis_index("feat") // 4
    own = exact[pl.ds(my_z, 1)][0]
    far = peer[pl.ds(pl.multiple_of(my_z * 4 * OWN, 4 * OWN), 2 * OWN), :].astype(F32)
    hiddens = []
    for value in (own, far):
        value = jnp.concatenate([value[0:OWN, :], value[OWN : 2 * OWN, :]], axis=1)
        hiddens.append((value * (0.5 + 0.5 * jnp.tanh(0.5 * value))).astype(BF16))
    ext[pl.ds(pl.multiple_of(my_graph * OWN, OWN), OWN), :] = hiddens[0]
    ext[pl.ds(pl.multiple_of((1 - my_graph) * OWN, OWN), OWN), :] = hiddens[1]
    mean = (dot(own_counts[...].astype(BF16), ext[...], ((1,), (0,))) / FAN2).astype(BF16)
    out = dot(hiddens[0], w_second[0], ((1,), (0,))) + dot(mean, w_second[1], ((1,), (0,)))
    layer_out[...] = out.astype(BF16)


def last_kernel(
    n_feat, plane_0, plane_1, plane_2, plane_3, w_second, x_mine, x_peer,
    own_counts, swapped, kept, cots, d_hidden, lists, spread, turn, hidden, d_pre, slices,
):
    write_back(n_feat, plane_0, plane_1, plane_2, plane_3, w_second, cots, d_hidden, own_counts, lists, spread, turn)
    my_graph = lax.axis_index("graph")
    my_feat = lax.axis_index("feat")
    rows = n_feat * OWN
    half = rows // 2
    line = n_feat // 4
    d_pre[...] = jnp.zeros_like(d_pre)
    my_y = my_feat // 2 % 2
    for (x, y), message in zip(PLANE, (plane_0, plane_1, plane_2, plane_3)):
        graph = my_graph ^ x
        for z in range(line):
            span = pl.ds(pl.multiple_of((graph * 2 + (my_y ^ y)) * LANES + z * OWN, OWN), OWN)
            top = 4 * z * OWN
            value = jnp.concatenate([message[top : top + OWN, :], message[top + OWN : top + 2 * OWN, :]], axis=1).astype(F32)
            sig = 0.5 + 0.5 * jnp.tanh(0.5 * value)
            hidden[span, :] = (value * sig).astype(BF16)
            slope = sig * (1.0 + value * (1.0 - sig))
            target = pl.ds(pl.multiple_of(graph * rows + (z * 4 + (my_feat % 4 ^ 2 * y)) * OWN, OWN), OWN)
            d_pre[target, :] = (d_hidden[span, :] * slope).astype(BF16)

    second = dot(hidden[...], cots[...], ((0,), (0,))).astype(BF16)
    swapped[0:HID, :] = second[:, 0:HID]
    swapped[HID : 2 * HID, :] = second[:, HID : 2 * HID]

    for z in range(line):
        cols = slice(z * LANES, (z + 1) * LANES)
        slices[0, :, cols] = x_mine[z]
        slices[1, :, cols] = x_peer[z]
    mine = d_pre[pl.ds(pl.multiple_of(my_graph * rows, rows), rows), :]
    peer = d_pre[pl.ds(pl.multiple_of((1 - my_graph) * rows, rows), rows), :]
    first = dot(slices[0], mine, ((1,), (0,))) + dot(slices[1], peer, ((1,), (0,)))
    kept[...] = first[0 : 2 * OWN, :]
    swapped[2 * HID : 2 * HID + 2 * OWN, :] = first[2 * OWN : 4 * OWN, :].astype(BF16)


def add_kernel(mine, theirs, kept, grad_second, grad_first):
    for w in range(2):
        span = slice(w * HID, (w + 1) * HID)
        grad_second[w] = mine[span, :].astype(F32) + theirs[span, :].astype(F32)
    grad_first[...] = kept[...] + theirs[2 * HID : 2 * HID + 2 * OWN, :].astype(F32)


VMEM = pl.BlockSpec(memory_space=pltpu.VMEM)
ANY = pl.BlockSpec(memory_space=pl.ANY)
SMEM = pl.BlockSpec(memory_space=pltpu.SMEM)
LIMIT = 40 * 1024 * 1024


def call(kernel, outs, ins, scratch=(), name=None, aliases=None):
    return pl.pallas_call(
        kernel,
        out_shape=[jax.ShapeDtypeStruct(shape, dtype) for shape, dtype in outs],
        in_specs=ins,
        out_specs=[VMEM] * len(outs),
        scratch_shapes=list(scratch),
        input_output_aliases=aliases or {},
        compiler_params=pltpu.CompilerParams(vmem_limit_bytes=LIMIT),
        name=name,
    )


def swap(n_feat, value, relative):
    return lax.ppermute(value, AXES, [(d, d ^ relative) for d in range(2 * n_feat)])


def pair_body(n_feat, features, w_first, w_second, cotangent, nbr_first, send_rows, nbr_second):
    devices = 2 * n_feat
    rows = n_feat * OWN
    width = 2 * OWN
    line = n_feat // 4
    from_hbm = [features.T, nbr_first.T, w_first.reshape(width, HID), cotangent, nbr_second.T, send_rows]
    block = (line, width, LANES)
    sources = features.shape[0]
    counts, feat_mine, w_mine, pack = call(
        count_kernel,
        [((sources, rows), BF16), ((OWN, sources), BF16), ((width, HID), BF16), ((width + INTS, LANES), BF16)],
        [ANY] * 6,
        [pltpu.VMEM(x.shape, x.dtype) for x in (nbr_first.T, cotangent, nbr_second.T)]
        + [pltpu.SMEM(send_rows.shape, jnp.int32), pltpu.SemaphoreType.DMA((6,))],
        name="count",
    )(*[pltpu.with_memory_space_constraint(x, pltpu.HBM) for x in from_hbm])
    x_mine, kept, sent = call(
        first_kernel,
        [((line, 2 * width, LANES), BF16), (block, F32), (block, BF16)],
        [VMEM] * 5,
        [pltpu.VMEM((rows, HID), F32)],
        name="first",
    )(counts, feat_mine, w_mine, swap(n_feat, from_hbm[0], 1), swap(n_feat, from_hbm[2], 1))
    x_peer = swap(n_feat, x_mine, n_feat)
    (message,) = call(
        sum_plane_kernel,
        [((line * width + width + INTS, LANES), BF16)],
        [VMEM] * 3,
        name="sum_plane",
    )(pack, kept, swap(n_feat, sent, 2))
    exact, message = call(
        sum_line_kernel,
        [(block, F32), ((2 * line * width + INTS, LANES), BF16)],
        [ANY] + [VMEM] * line,
        name="sum_line",
    )(x_peer, message, *[swap(n_feat, message, 4 * z) for z in (1, 3, 2)])
    plane = [swap(n_feat, message, r) for r in (n_feat + 2, 2, n_feat)]
    plane = [message, *plane[::-1]]

    half = (devices // 2) * OWN
    own_counts, swapped, kept = call(
        functools.partial(last_kernel, n_feat),
        [((OWN, width), F32), ((2 * HID + width, HID), BF16), ((width, HID), F32)],
        [VMEM] * 7,
        [
            pltpu.VMEM((half, 2 * HID), BF16),
            pltpu.VMEM((half, HID), F32),
            pltpu.VMEM((4, INTS, LANES), BF16),
            pltpu.VMEM((4, width, LANES), F32),
            pltpu.VMEM((LANES, width), F32),
            pltpu.VMEM((half, HID), BF16),
            pltpu.VMEM((2 * half, HID), BF16),
            pltpu.VMEM((2, 2 * width, rows), BF16),
        ],
        name="last",
    )(*plane, w_second, x_mine, x_peer)
    (layer_out,) = call(
        functools.partial(out_kernel, n_feat),
        [((OWN, HID), BF16)],
        [VMEM] * 4,
        [pltpu.VMEM((width, HID), BF16)],
        name="out",
    )(plane[1], exact, own_counts, w_second)
    grad_second, grad_first = call(
        add_kernel,
        [((2, HID, HID), F32), ((width, HID), F32)],
        [VMEM] * 3,
        name="add",
    )(swapped, swap(n_feat, swapped, 1), kept)
    return (layer_out, grad_second, grad_first.reshape(2, OWN, HID))


def body(features, w_first, w_second, cotangent, nbr_first, send_rows, nbr_second):
    high = lax.Precision.HIGHEST
    targets = nbr_first.shape[0]
    gathered = features[nbr_first].astype(F32)
    mean_all = (jnp.sum(gathered, axis=1) / FAN1).astype(BF16)
    self_all = features[:targets]
    term = jnp.dot(self_all, w_first[0], preferred_element_type=F32)
    pre_one = lax.psum_scatter(
        term + jnp.dot(mean_all, w_first[1], preferred_element_type=F32),
        "feat",
        scatter_dimension=0,
        tiled=True,
    )
    hidden = jax.nn.silu(pre_one).astype(BF16)
    slot_rows = send_rows[0]
    valid = (slot_rows >= 0)[..., None]
    picked = hidden[jnp.maximum(slot_rows, 0)]
    outgoing_rows = jnp.where(valid, picked, jnp.zeros_like(picked))
    received = lax.all_to_all(outgoing_rows, "graph", split_axis=0, concat_axis=0, tiled=True)
    ext = jnp.concatenate([hidden, received.reshape(-1, HID)], axis=0)
    width = ext.shape[0]
    counts = jnp.zeros((OWN, width), F32)
    for k in range(FAN2):
        counts = counts + (nbr_second[:, k, None] == jnp.arange(width)[None, :]).astype(F32)
    mean_two = (jnp.dot(counts.astype(BF16), ext, preferred_element_type=F32) / FAN2).astype(BF16)
    layer_out = jnp.dot(hidden, w_second[0], preferred_element_type=F32)
    layer_out = (layer_out + jnp.dot(mean_two, w_second[1], preferred_element_type=F32)).astype(BF16)
    grad_terms = jnp.stack(
        [
            jnp.einsum("rh,ro->ho", hidden, cotangent, preferred_element_type=F32),
            jnp.einsum("rh,ro->ho", mean_two, cotangent, preferred_element_type=F32),
        ]
    )
    grad_second = lax.psum(grad_terms, AXES)
    d_self = jnp.einsum("ro,ho->rh", cotangent, w_second[0], preferred_element_type=F32)
    d_mean = jnp.einsum("ro,ho->rh", cotangent, w_second[1], preferred_element_type=F32) / FAN2
    d_ext = jnp.dot(counts.T, d_mean, precision=high)
    halo_grad = d_ext[OWN:].reshape(-1, slot_rows.shape[1], HID).astype(BF16)
    returned = lax.all_to_all(halo_grad, "graph", split_axis=0, concat_axis=0, tiled=True)
    onehot = (slot_rows.reshape(-1)[:, None] == jnp.arange(OWN)[None, :]).astype(BF16)
    d_back = jnp.einsum("sr,sh->rh", onehot, returned.reshape(-1, HID), preferred_element_type=F32)
    d_hidden = d_self + d_ext[:OWN] + d_back
    d_pre = (d_hidden * silu_grad(pre_one)).astype(BF16)
    piece = lax.all_gather(d_pre, "feat", axis=0, tiled=True)
    first_sum = jnp.einsum("rf,rh->fh", self_all, piece, preferred_element_type=F32)
    second_sum = jnp.einsum("rf,rh->fh", mean_all, piece, preferred_element_type=F32)
    grad_first = lax.psum(jnp.stack([first_sum, second_sum]), "graph")
    return (layer_out, grad_second, grad_first)


def solution(mesh):
    n_graph = mesh.shape["graph"]
    n_feat = mesh.shape["feat"]
    in_specs = (
        P("graph", "feat"),
        P(None, "feat", None),
        P(),
        P(AXES, None),
        P("graph", None),
        P(AXES, None, None),
        P(AXES, None),
    )
    out_specs = (P(AXES, None), P(), P(None, "feat", None))
    two = n_graph == 2 and n_feat == 16
    chosen = functools.partial(pair_body, n_feat) if two else body
    return jax.shard_map(chosen, mesh=mesh, in_specs=in_specs, out_specs=out_specs, check_vma=False)
```
